128 devices in a mesh: tm: 16 (over y, x_hi, core), inch: 8 (over z, x_lo).
Axes of the slice: x: 4 (x_hi: 2, x_lo: 2; x = x_hi * 2 + x_lo), y: 4, z: 4, core: 2. Of those that a mesh axis runs over, the one named last changes fastest.
Arguments:
- signal: bfloat16 [32768, 128], P('tm', 'inch'), may hold values from -6 to 6
- response: bfloat16 [32768, 256], P('tm'), may hold values from -6 to 6
- kernel: float32 [256, 128, 256], P('tm', 'inch'), may hold values from -16 to 16
Outputs:
- kernel_out: float32 [256, 128, 256], P('tm', 'inch')
- residual: bfloat16 [32768, 256], P('tm', 'inch')
The draws below stay inside these ranges and needn't reach their ends.
All inputs are finite; a program needn't handle non-finite values.
Results may differ from the reference program's by a relative error of at most 0.024.
Values may be sent and summed in bfloat16 or wider, within the bound.
A program may use at most 576 MiB of HBM per device.

```python
import math
import jax
import jax.numpy as jnp
from jax import lax

TAPS = 256
CI = 128
CO = 256
ITERS = 2
NT = 32768


def shaped_taps(base, tap_ratio, chan_ratio):
    tap_pos = jnp.arange(TAPS, dtype=jnp.float32) / max(TAPS - 1, 1) - 0.5
    chan_pos = jnp.arange(CI, dtype=jnp.float32) / max(CI - 1, 1) - 0.5
    tap_scale = jnp.exp(math.log(tap_ratio) * tap_pos)[:, None, None]
    chan_scale = jnp.exp(math.log(chan_ratio) * chan_pos)[None, :, None]
    return jnp.clip(base * tap_scale * chan_scale, -16.0, 16.0)


def draw_kernel(key, part):
    key = jax.random.fold_in(key, 7)
    base = jnp.clip(jax.random.normal(key, (TAPS, CI, CO), jnp.float32), -6.0, 6.0)
    return shaped_taps(base, 4.0, 2.0)


def levels(rng, shape, split, low, top_value):
    def one(axis_at, shards_of):
        heights = jax.random.uniform(jax.random.fold_in(jax.random.fold_in(rng, 6), axis_at), (shards_of,), jnp.float32, low / len(split), top_value / len(split))
        return jnp.repeat(jnp.exp(heights), shape[axis_at] // shards_of).reshape((-1,) + (1,) * (len(shape) - axis_at - 1))

    factor_of = one(*split[0])
    for cut in split[1:]:
        factor_of = factor_of * one(*cut)
    return factor_of


def normal_values(key, shape, scale, limit, pieces=(), held_as=jnp.bfloat16):
    values = scale * jax.random.normal(key, shape, jnp.float32)
    if pieces:
        values = values * levels(key, shape, pieces, -0.22, 0.18)
    return jnp.clip(values, -limit, limit).astype(held_as)


def setup_inputs(seed: int = 0) -> dict:
    key_of = jax.random.split(jax.random.key(seed), 4)
    return {
        "signal": normal_values(key_of[0], (NT, CI), 1.0, 6.0, ((0, 16), (1, 8))),
        "response": normal_values(key_of[1], (NT, CO), 1.0, 6.0, ((0, 16),)),
        "kernel": draw_kernel(jax.random.fold_in(key_of[3], 71), 0),
    }


STEP_SIZE = 0.5
EPSILON = 1e-06

def reference(signal, response, kernel):
    total_rows = signal.shape[0]
    fft_length = total_rows + TAPS
    scale = 1.0 / math.sqrt(TAPS * CI)
    spec_signal = jnp.fft.rfft(signal.astype(jnp.float32), n=fft_length, axis=0)
    target = response.astype(jnp.float32)
    residual = response
    for sweep in range(ITERS):
        weights = kernel.astype(jnp.bfloat16).astype(jnp.float32)

        def add_channel(carry, inputs):
            column, taps_here = inputs
            return (carry + column[:, None] * jnp.fft.rfft(taps_here, n=fft_length, axis=0), None)
        start_spec = jnp.zeros((fft_length // 2 + 1, CO), spec_signal.dtype)
        spec_pred = lax.scan(add_channel, start_spec, (spec_signal.T, jnp.transpose(weights, (1, 0, 2))))[0]
        predicted = jnp.fft.irfft(spec_pred, n=fft_length, axis=0)[:total_rows] * scale
        residual = (target - predicted).astype(jnp.bfloat16)
        spec_resid = jnp.fft.rfft(residual.astype(jnp.float32), n=fft_length, axis=0)

        def correlate(column):
            return jnp.fft.irfft(jnp.conj(column)[:, None] * spec_resid, n=fft_length, axis=0)[:TAPS]
        gradient = jnp.transpose(lax.map(correlate, spec_signal.T), (1, 0, 2)) * scale
        energy = jnp.sum(gradient * gradient)
        kernel = kernel + STEP_SIZE * gradient * lax.rsqrt(energy / (TAPS * CI * CO) + EPSILON)
    return (kernel, residual)
```

```python
import math

import jax
import jax.numpy as jnp
from jax import lax
from jax.experimental import pallas as pl
from jax.experimental.pallas import tpu as pltpu
from jax.sharding import PartitionSpec as P

STEP_SIZE = 0.5
EPSILON = 1e-06
F32 = jnp.float32
BF16 = jnp.bfloat16
MESH = pl.DeviceIdType.MESH
TAPS = 256
CI = 128
CO = 256
SCALE = 1.0 / math.sqrt(TAPS * CI)
COUNT = TAPS * CI * CO


def remote(src, dst, send, recv, device):
    return pltpu.make_async_remote_copy(
        src_ref=src, dst_ref=dst, send_sem=send, recv_sem=recv,
        device_id=device, device_id_type=MESH,
    )


def body(
    sig_ref, tail_ref, ker_ref, resp_ref,
    step_ref, resid_ref,
    pieces, halo_in, perm, sb, xe, weights, response, r_even, r_odd,
    grad_out, grad_in, grad_own, grad_all, tiles, energy_a, energy_b, energy_own, acc, resid_all,
    resid_in,
    ker_send, ker_recv, resp_send, resp_recv, tail_send, tail_recv,
    z_send, z_recv, zh_send, zh_recv, x_send, x_recv, c_send, c_recv,
    w_send, w_recv, rs_send, rs_recv, ag_send, ag_recv,
    ea_send, ea_recv, eb_send, eb_recv, t_send, t_recv, o_send, o_recv,
):
    tm = lax.axis_index("tm")
    inch = lax.axis_index("inch")
    y = tm // 4
    s = tm % 4
    x_hi = s // 2
    core = s % 2
    z = inch // 2
    x_lo = inch % 2
    x = x_hi * 2 + x_lo
    rank = inch * 4 + s

    def in_plane(d):
        return (y * 4 + d % 4, d // 4)

    def along_y(r):
        return ((((y + r) % 4) * 4) + s, inch)

    def along_z(r):
        return (tm, ((z + r) % 4) * 2 + x_lo)

    def along_x(r):
        there = (x + r) % 4
        return (y * 4 + (there // 2) * 2 + core, z * 2 + there % 2)

    def in_group(r):
        return (y * 4 + (s + r) % 4, inch)

    barrier = pltpu.get_barrier_semaphore()

    def greet(r, carry):
        pl.semaphore_signal(
            barrier, inc=1, device_id=in_plane((rank + r) % 32), device_id_type=MESH
        )
        return carry

    lax.fori_loop(1, 32, greet, 0)
    for r in (1, 2, 3):
        pl.semaphore_signal(barrier, inc=1, device_id=along_y(r), device_id_type=MESH)
    pl.semaphore_signal(
        barrier, inc=1, device_id=((tm + 15) % 16, inch), device_id_type=MESH
    )

    lane_z = pl.ds(pl.multiple_of(z * 128, 128), 128)
    pieces[x_hi, core, x_lo, 0:256, lane_z] = sig_ref[...]

    pl.semaphore_wait(barrier, 35)

    tail_copy = remote(tail_ref, halo_in, tail_send, tail_recv, ((tm + 1) % 16, inch))
    tail_copy.start()
    z_copies = []
    for r in (1, 2, 3):
        view = pieces.at[x_hi, core, x_lo, pl.ds(0, 256), lane_z]
        z_copies.append(remote(view, view, z_send.at[r - 1], z_recv.at[r - 1], along_z(r)))
        z_copies[-1].start()

    row_k = pl.multiple_of((s // 2) * 128 + inch * 16, 16)
    lane_k = pl.multiple_of((s % 2) * 128, 128)

    def send_taps(r, carry):
        d = (rank + r) % 32
        remote(
            ker_ref.at[d], weights.at[y, pl.ds(row_k, 16), pl.ds(lane_k, 128)],
            ker_send, ker_recv, in_plane(d),
        ).start()
        return carry

    lax.fori_loop(1, 32, send_taps, 0)
    weights[y, pl.ds(row_k, 16), pl.ds(lane_k, 128)] = ker_ref[rank]

    tail_copy.wait()
    pieces[x_hi, core, x_lo, 256:288, lane_z] = halo_in[...]
    zh_copies = []
    for r in (1, 2, 3):
        view = pieces.at[x_hi, core, x_lo, pl.ds(256, 32), lane_z]
        zh_copies.append(remote(view, view, zh_send.at[r - 1], zh_recv.at[r - 1], along_z(r)))
        zh_copies[-1].start()

    rows_s = pl.ds(pl.multiple_of(s * 8, 8), 8)
    resp_copies = []
    for r in (1, 2, 3):
        resp_copies.append(remote(
            resp_ref.at[(s + r) % 4], response.at[:, rows_s, :],
            resp_send.at[r - 1], resp_recv.at[r - 1], in_group(r),
        ))
        resp_copies[-1].start()
    response[:, rows_s, :] = resp_ref[s]

    row = lax.broadcasted_iota(jnp.int32, (1024, 128), 0)
    lane = lax.broadcasted_iota(jnp.int32, (1024, 128), 1)
    for e in range(8):
        src = (lane // 16) % 2 * 512 + (lane // 32) * 128 + e * 16 + lane % 16
        perm[:, e * 128:(e + 1) * 128] = jnp.where(row == src, 1.0, 0.0).astype(BF16)

    all_tiles = ker_ref.at[pl.ds(0, 31)]
    pltpu.make_async_copy(all_tiles, all_tiles, ker_recv).wait()
    w_copies = []
    for r in (2, 1, 3):
        w_copies.append(remote(
            weights.at[y], weights.at[y], w_send.at[r - 1], w_recv.at[r - 1], along_y(r)
        ))
        w_copies[-1].start()

    other = (y * 4 + x_hi * 2 + 1 - core, inch)
    for copy in z_copies + zh_copies:
        copy.wait()
    x_copies = []
    for r in (2, 1, 3):
        view = pieces.at[x_hi, core, x_lo]
        x_copies.append(remote(view, view, x_send.at[r - 1], x_recv.at[r - 1], along_x(r)))
        x_copies[-1].start()
    c_copies = []
    for r in (0, 3, 1, 2):
        there = (x + 4 - r) % 4
        view = pieces.at[there // 2, core, there % 2]
        if r:
            x_copies[{2: 0, 1: 1, 3: 2}[r]].wait_recv()
        c_copies.append(remote(view, view, c_send.at[r], c_recv.at[r], other))
        c_copies[-1].start()
    for copy in c_copies:
        copy.wait_recv()

    at_start = y == 0
    halo = jnp.dot(
        jnp.concatenate([pieces[0, 0, 0, 256:288, :], pieces[0, 0, 1, 256:288, :]], axis=1),
        perm[...], preferred_element_type=F32,
    )
    halo = jnp.where(at_start, 0.0, halo)
    acc[0:128, 0:256] = jnp.concatenate(
        [halo[:, 256 * j:256 * (j + 1)] for j in range(4)], axis=0
    )
    for p1 in range(4):
        for e in range(8):
            for q in range(8):
                half = e % 2
                xe[p1 * 8 + e:p1 * 8 + e + 1, q * 128:(q + 1) * 128] = acc[
                    pl.ds((e // 2) * 32 + p1 * 8 + 7 - q, 1), half * 128:(half + 1) * 128
                ]
    first = lax.broadcasted_iota(jnp.int32, (256, 128), 0) % 32 == 0
    for p1 in range(4):
        stacked = jnp.concatenate(
            [
                jnp.concatenate(
                    [pieces[g // 2, g % 2, lo, p1 * 64:(p1 + 1) * 64, :] for lo in range(2)],
                    axis=1,
                )
                for g in range(4)
            ],
            axis=0,
        )
        for e in range(8):
            block = jnp.dot(
                stacked, perm[:, e * 128:(e + 1) * 128], preferred_element_type=F32
            )
            block = block.reshape(4, 8, 8, 128).transpose(1, 0, 2, 3).reshape(256, 128)
            edge = halo[p1 * 8:(p1 + 1) * 8, e * 128:(e + 1) * 128]
            edge = jnp.broadcast_to(edge[:, None, :], (8, 32, 128)).reshape(256, 128)
            before = jnp.where(first, edge, pltpu.roll(block, 1, axis=0))
            sb[p1 * 8 + e, 256:512, :] = block.astype(BF16)
            sb[p1 * 8 + e, 0:256, :] = before.astype(BF16)

    for copy in w_copies + resp_copies:
        copy.wait()

    wide_lane = lax.broadcasted_iota(jnp.int32, (256, 256), 1)
    wide_row = lax.broadcasted_iota(jnp.int32, (256, 256), 0)
    ext_lane = lax.broadcasted_iota(jnp.int32, (32, 256), 1)
    ext_row = lax.broadcasted_iota(jnp.int32, (32, 256), 0)

    def tap_matrix():
        return jnp.concatenate([weights[j] for j in range(4)], axis=0)

    def forward():
        acc[...] = jnp.zeros_like(acc)

        def group(g, carry):
            lhs = jnp.concatenate(
                [
                    jnp.concatenate(
                        [sb[g * 4 + j, (8 - q) * 32:(8 - q) * 32 + 256, :] for q in range(8)],
                        axis=1,
                    )
                    for j in range(4)
                ],
                axis=0,
            )
            product = jnp.dot(lhs, tap_matrix(), preferred_element_type=F32)
            here = acc[0:256, :]
            after = acc[256:512, :]
            for j in range(4):
                shift = (g * 4 + j) * 8
                turned = pltpu.roll(product[j * 256:(j + 1) * 256], shift, axis=1)
                keep = wide_lane >= shift
                here = here + jnp.where(keep, turned, 0.0)
                after = after + jnp.where(keep, 0.0, turned)
            acc[0:256, :] = here
            acc[256:512, :] = after
            return carry

        lax.fori_loop(0, 8, group, 0)
        edge = jnp.dot(xe[...].astype(BF16), tap_matrix(), preferred_element_type=F32)
        edge = pltpu.roll(edge, 0, axis=1, stride=8, stride_axis=0)
        edge = jnp.sum(jnp.where(ext_lane < ext_row * 8, edge, 0.0), axis=0, keepdims=True)
        after = acc[256:512, :]
        moved = jnp.where(
            wide_row >= 32, pltpu.roll(after, 32, axis=0), pltpu.roll(after, 33, axis=0)
        )
        moved = jnp.where(wide_row == 0, jnp.broadcast_to(edge, (256, 256)), moved)
        return (acc[0:256, :] + moved) * SCALE

    def expand(resid):
        later = jnp.where(
            wide_row < 224, pltpu.roll(resid, 224, axis=0), pltpu.roll(resid, 223, axis=0)
        )
        later = jnp.where(wide_row == 255, 0.0, later)
        here_t = resid.T
        later_t = later.T
        both = jnp.concatenate([here_t, later_t], axis=0)
        r_even[...] = both.astype(BF16)
        r_odd[...] = jnp.concatenate([both[8:], both[:8]], axis=0).astype(BF16)

    def edge_windows(resid):
        line = jnp.broadcast_to(resid[0:1, :], (32, 256))
        line = pltpu.roll(line, 8, axis=1, stride=8, stride_axis=0)
        return jnp.where(ext_lane + (31 - ext_row) * 8 >= 256, line, 0.0)

    def gradient_of(there, edges):
        total = jnp.zeros((256, 256), F32)
        top = pl.multiple_of((8 - 2 * there) * 32, 32)
        low = pl.multiple_of((7 - 2 * there) * 32, 32)
        for g in range(8):
            left = []
            right = []
            for p in range(4 * g, 4 * g + 4):
                windows = r_odd if p % 2 else r_even
                at = 8 * (p - p % 2)
                left.append(windows[at:at + 256, :])
                right.append(jnp.concatenate(
                    [sb[p, pl.ds(top, 256), :], sb[p, pl.ds(low, 256), :]], axis=1
                ))
            total = total + jnp.dot(
                jnp.concatenate(left, axis=1), jnp.concatenate(right, axis=0),
                preferred_element_type=F32,
            )
        lanes = pl.ds(pl.multiple_of(there * 256, 256), 256)
        total = total + jnp.dot(edges, xe[:, lanes].astype(BF16), preferred_element_type=F32)
        return total.T * SCALE

    def send_energy(turn):
        energy_own[turn, 0] = jnp.full((8, 128), jnp.sum(grad_own[...] * grad_own[...]), F32)

        def send(r, carry):
            remote(
                energy_own.at[turn, 0], energy_a.at[turn, r - 1],
                ea_send.at[turn], ea_recv.at[turn], in_plane((rank + r) % 32),
            ).start()
            return carry

        lax.fori_loop(1, 32, send, 0)

    def send_tiles(turn):

        def send(r, carry):
            d = (rank + r) % 32
            rows = pl.ds(pl.multiple_of(((d % 4) // 2) * 128 + (d // 4) * 16, 16), 16)
            lanes = pl.ds(pl.multiple_of((d % 2) * 128, 128), 128)
            remote(
                grad_all.at[turn, y, rows, lanes], tiles.at[turn, rank],
                t_send.at[turn], t_recv.at[turn], in_plane(d),
            ).start()
            return carry

        lax.fori_loop(1, 32, send, 0)
        tiles[turn, rank] = grad_all[turn, y, pl.ds(row_k, 16), pl.ds(lane_k, 128)]

    def finish_energy(turn):
        mine = energy_a.at[turn]
        pltpu.make_async_copy(mine, mine, ea_recv.at[turn]).wait()
        energy_own[turn, 1] = energy_own[turn, 0] + jnp.sum(energy_a[turn], axis=0)
        copies = []
        for r in (1, 2, 3):
            copies.append(remote(
                energy_own.at[turn, 1], energy_b.at[turn, r - 1],
                eb_send.at[turn, r - 1], eb_recv.at[turn, r - 1], along_y(r),
            ))
            copies[-1].start()
        for copy in copies:
            copy.wait_recv()
        total = energy_own[turn, 1] + jnp.sum(energy_b[turn], axis=0)
        factor = STEP_SIZE * lax.rsqrt(total / COUNT + EPSILON)
        return factor[0:1, :], copies

    factors = []
    pending = []
    for turn in range(2):
        predicted = forward()
        resid = (response[...].reshape(256, 256) - predicted).astype(BF16).astype(F32)
        if turn == 1:
            resid_all[...] = resid.reshape(8, 32, 256)
            for r in (1, 2, 3):
                there = pl.ds(pl.multiple_of(((s + r) % 4) * 8, 8), 8)
                pending.append(remote(
                    resid_all.at[:, there, :], resid_in.at[s],
                    o_send.at[r - 1], o_recv.at[r - 1], in_group(r),
                ))
                pending[-1].start()
        expand(resid)
        flipped = edge_windows(resid)
        edges = jnp.concatenate(
            [flipped[31 - j:32 - j, :] for j in range(32)], axis=0
        ).T.astype(BF16)
        rs_copies = []
        for r in (2, 1, 3):
            grad_out[r - 1] = gradient_of((y + r) % 4, edges).astype(BF16)
            rs_copies.append(remote(
                grad_out.at[r - 1], grad_in.at[r - 1],
                rs_send.at[turn, r - 1], rs_recv.at[turn, r - 1], along_y(r),
            ))
            rs_copies[-1].start()
        own = gradient_of(y, edges)
        for copy in rs_copies:
            copy.wait()
        for r in range(3):
            own = own + grad_in[r].astype(F32)
        grad_own[...] = own
        grad_all[turn, y] = own.astype(BF16)
        ag_copies = []
        if turn == 0:
            for r in (2, 1, 3):
                ag_copies.append(remote(
                    grad_all.at[turn, y], grad_all.at[turn, y],
                    ag_send.at[r - 1], ag_recv.at[r - 1], along_y(r),
                ))
                ag_copies[-1].start()
        send_energy(turn)
        send_tiles(turn)
        factor, copies = finish_energy(turn)
        factors.append(factor)
        pending += [("send", copy) for copy in copies]
        if turn == 0:
            for copy in ag_copies:
                copy.wait()
            wide = jnp.concatenate([factor, factor], axis=1)
            for j in range(4):
                weights[j] = (
                    weights[j].astype(F32) + wide * grad_all[0, j].astype(F32)
                ).astype(BF16)

    for turn in range(2):
        half = tiles.at[turn, pl.ds(0, 31)]
        pltpu.make_async_copy(half, half, t_recv.at[turn]).wait()
    step_ref[...] = (
        factors[0] * tiles[0].astype(F32) + factors[1] * tiles[1].astype(F32)
    )
    for item in pending:
        if isinstance(item, tuple):
            item[1].wait_send()
        else:
            item.wait()
    resid_ref[...] = resid_in[...]
    resid_ref[s] = resid_all[:, rows_s, :]

    pltpu.make_async_copy(all_tiles, all_tiles, ker_send).wait()
    for copy in x_copies + c_copies:
        copy.wait_send()
    for turn in range(2):
        mine = energy_a.at[turn]
        pltpu.make_async_copy(mine, mine, ea_send.at[turn]).wait()
        half = tiles.at[turn, pl.ds(0, 31)]
        pltpu.make_async_copy(half, half, t_send.at[turn]).wait()


def local(signal, response, kernel):
    inch = lax.axis_index("inch")
    sig = signal.reshape(8, 8, 4, 8, 16).transpose(2, 1, 0, 3, 4)
    tail = sig[:, :, 7].reshape(32, 128)
    sig = sig.reshape(256, 128)
    ker = kernel.astype(BF16).reshape(16, 16, 32, 8).transpose(2, 1, 0, 3).reshape(32, 16, 128)
    resp = lax.dynamic_slice_in_dim(response, inch * 32, 32, 1).astype(F32)
    resp = resp.reshape(8, 8, 32, 4, 8).transpose(3, 1, 0, 2, 4).reshape(4, 8, 8, 256)
    dma = pltpu.SemaphoreType.DMA
    vmem = pl.BlockSpec(memory_space=pltpu.VMEM)
    step, resid = pl.pallas_call(
        body,
        out_shape=(
            jax.ShapeDtypeStruct((32, 16, 128), F32),
            jax.ShapeDtypeStruct((4, 8, 8, 256), F32),
        ),
        in_specs=[vmem] * 4,
        out_specs=(vmem, vmem),
        scratch_shapes=[
            pltpu.VMEM((2, 2, 2, 288, 512), BF16),
            pltpu.VMEM((32, 128), BF16),
            pltpu.VMEM((1024, 1024), BF16),
            pltpu.VMEM((32, 512, 128), BF16),
            pltpu.VMEM((32, 1024), F32),
            pltpu.VMEM((4, 256, 256), BF16),
            pltpu.VMEM((8, 32, 256), F32),
            pltpu.VMEM((512, 256), BF16),
            pltpu.VMEM((512, 256), BF16),
            pltpu.VMEM((3, 256, 256), BF16),
            pltpu.VMEM((3, 256, 256), BF16),
            pltpu.VMEM((256, 256), F32),
            pltpu.VMEM((2, 4, 256, 256), BF16),
            pltpu.VMEM((2, 32, 16, 128), BF16),
            pltpu.VMEM((2, 31, 8, 128), F32),
            pltpu.VMEM((2, 3, 8, 128), F32),
            pltpu.VMEM((2, 2, 8, 128), F32),
            pltpu.VMEM((512, 256), F32),
            pltpu.VMEM((8, 32, 256), F32),
            pltpu.VMEM((4, 8, 8, 256), F32),
            dma, dma, dma((3,)), dma((3,)), dma, dma,
            dma((3,)), dma((3,)), dma((3,)), dma((3,)), dma((3,)), dma((3,)), dma((4,)), dma((4,)),
            dma((3,)), dma((3,)), dma((2, 3)), dma((2, 3)), dma((3,)), dma((3,)),
            dma((2,)), dma((2,)), dma((2, 3)), dma((2, 3)), dma((2,)), dma((2,)), dma((3,)), dma((3,)),
        ],
        compiler_params=pltpu.CompilerParams(
            collective_id=0, has_side_effects=True, vmem_limit_bytes=60 * 2**20
        ),
    )(sig, tail, ker, resp)
    kernel_out = kernel + step.reshape(32, 16, 16, 8).transpose(2, 1, 0, 3).reshape(16, 16, 256)
    resid = resid.astype(BF16).reshape(4, 8, 8, 32, 8).transpose(2, 1, 3, 0, 4).reshape(2048, 32)
    return kernel_out, resid


def solution(mesh):
    placed = (P("tm", "inch"), P("tm", None), P("tm", "inch", None))
    return jax.shard_map(
        local,
        mesh=mesh,
        in_specs=placed,
        out_specs=(P("tm", "inch", None), P("tm", "inch")),
        check_vma=False,
    )
```

```python
import math

import jax
import jax.numpy as jnp
from jax import lax
from jax.experimental import pallas as pl
from jax.experimental.pallas import tpu as pltpu
from jax.sharding import PartitionSpec as P

STEP_SIZE = 0.5
EPSILON = 1e-06
F32 = jnp.float32
BF16 = jnp.bfloat16
MESH = pl.DeviceIdType.MESH
TAPS = 256
CI = 128
CO = 256
SCALE = 1.0 / math.sqrt(TAPS * CI)
COUNT = TAPS * CI * CO


def remote(src, dst, send, recv, device):
    return pltpu.make_async_remote_copy(
        src_ref=src, dst_ref=dst, send_sem=send, recv_sem=recv,
        device_id=device, device_id_type=MESH,
    )


def swap_blocks(parts):
    parts = list(parts)
    for bit in (1, 2, 4, 8):
        parts = swap_stage(parts, bit)
    return parts


def swap_stage(parts, bit):
    lane = lax.broadcasted_iota(jnp.int32, parts[0].shape, 1)
    high = (lane & (8 * bit)) != 0
    result = list(parts)
    for i in range(len(parts)):
        if not i & bit:
            low_part, high_part = parts[i], parts[i | bit]
            result[i] = jnp.where(high, pltpu.roll(high_part, 8 * bit, axis=1), low_part)
            result[i | bit] = jnp.where(
                high, high_part, pltpu.roll(low_part, 128 - 8 * bit, axis=1)
            )
    return result


def body(
    sig_ref, resp_hbm, ker_ref,
    kernel_ref, resid_ref,
    gathered, rows, ker_tiles, resp_raw, resp_wide, resp_out, resid_wide, base,
    sb, xe, weights, response, r_even, r_odd,
    grad_out, grad_in, grad_own, grad_all, tiles, energy_a, energy_b, energy_own, acc, resid_all,
    resid_in,
    hbm_sem, ker_send, ker_recv, resp_send, resp_recv, tail_send, tail_recv,
    za_send, za_recv, zh_send, zh_recv, xb_send, xb_recv, xa_send, xa_recv,
    zb_send, zb_recv, ca_send, ca_recv, cb_send, cb_recv,
    w_send, w_recv, rs_send, rs_recv, ag_send, ag_recv,
    ea_send, ea_recv, eb_send, eb_recv, t_send, t_recv, o_send, o_recv,
):
    tm = lax.axis_index("tm")
    inch = lax.axis_index("inch")
    y = tm // 4
    s = tm % 4
    x_hi = s // 2
    core = s % 2
    z = inch // 2
    x_lo = inch % 2
    x = x_hi * 2 + x_lo
    rank = inch * 4 + s

    def in_plane(d):
        return (y * 4 + d % 4, d // 4)

    def along_y(r):
        return ((((y + r) % 4) * 4) + s, inch)

    def along_z(r):
        return (tm, ((z + r) % 4) * 2 + x_lo)

    def along_x(r):
        there = (x + r) % 4
        return (y * 4 + (there // 2) * 2 + core, z * 2 + there % 2)

    def in_group(r):
        return (y * 4 + (s + r) % 4, inch)

    barrier = pltpu.get_barrier_semaphore()

    def greet(r, carry):
        pl.semaphore_signal(
            barrier, inc=1, device_id=in_plane((rank + r) % 32), device_id_type=MESH
        )
        return carry

    lax.fori_loop(1, 32, greet, 0)
    for r in (1, 2, 3):
        pl.semaphore_signal(barrier, inc=1, device_id=along_y(r), device_id_type=MESH)
    pl.semaphore_signal(
        barrier, inc=1, device_id=((tm + 15) % 16, inch), device_id_type=MESH
    )

    columns = pl.ds(pl.multiple_of((inch // 4) * 128, 128), 128)
    fetch = pltpu.make_async_copy(resp_hbm.at[:, columns], resp_raw, hbm_sem)
    fetch.start()
    row_z = pl.ds(pl.multiple_of(z * 16, 16), 16)
    gathered[x_hi, core, x_lo, row_z, 256:2304] = sig_ref[...]
    part_h, part_a, part_b = pl.ds(0, 256), pl.ds(256, 1024), pl.ds(1280, 1024)
    part_ha = pl.ds(0, 1280)

    pl.semaphore_wait(barrier, 35)

    nxt = (tm + 1) % 16
    tail_copy = remote(
        sig_ref.at[:, pl.ds(1792, 256)],
        gathered.at[(nxt % 4) // 2, nxt % 2, x_lo, row_z, part_h],
        tail_send, tail_recv, (nxt, inch),
    )
    tail_copy.start()
    za_copies = []
    xb_copies = []
    for r in (2, 1, 3):
        view = gathered.at[x_hi, core, x_lo, row_z, part_a]
        za_copies.append(remote(view, view, za_send.at[r - 1], za_recv.at[r - 1], along_z(r)))
        za_copies[-1].start()
        view = gathered.at[x_hi, core, x_lo, row_z, part_b]
        xb_copies.append(remote(view, view, xb_send.at[r - 1], xb_recv.at[r - 1], along_x(r)))
        xb_copies[-1].start()

    for half in range(2):
        swapped = swap_blocks([ker_ref[u, :, half * 128:(half + 1) * 128] for u in range(16)])
        for d in range(16):
            ker_tiles[half * 16 + d] = swapped[d].astype(BF16)
    row_k = pl.multiple_of((s // 2) * 128 + x_lo * 64 + z * 16, 16)
    lane_k = pl.multiple_of((s % 2) * 128, 128)

    def send_taps(r, carry):
        d = (rank + r) % 32
        remote(
            ker_tiles.at[d], weights.at[y, pl.ds(row_k, 16), pl.ds(lane_k, 128)],
            ker_send, ker_recv, in_plane(d),
        ).start()
        return carry

    lax.fori_loop(1, 32, send_taps, 0)
    weights[y, pl.ds(row_k, 16), pl.ds(lane_k, 128)] = ker_tiles[rank]

    tail_copy.wait()
    zh_copies = []
    for r in (2, 1, 3):
        view = gathered.at[x_hi, core, x_lo, row_z, part_h]
        zh_copies.append(remote(view, view, zh_send.at[r - 1], zh_recv.at[r - 1], along_z(r)))
        zh_copies[-1].start()

    other = (y * 4 + x_hi * 2 + 1 - core, inch)
    zb_copies = {}

    def pass_b(r):
        there = (x + 4 - r) % 4
        for k in (2, 1, 3):
            view = gathered.at[there // 2, core, there % 2, row_z, part_b]
            copy = remote(view, view, zb_send.at[r, k - 1], zb_recv.at[r, k - 1], along_z(k))
            copy.start()
            zb_copies[r, k] = copy

    place = {2: 0, 1: 1, 3: 2}
    pass_b(0)
    for copy in za_copies + zh_copies:
        copy.wait_recv()
    xa_copies = []
    for r in (2, 1, 3):
        view = gathered.at[x_hi, core, x_lo, :, part_ha]
        xa_copies.append(remote(view, view, xa_send.at[r - 1], xa_recv.at[r - 1], along_x(r)))
        xa_copies[-1].start()
    for r in (1, 3, 2):
        xb_copies[place[r]].wait_recv()
        pass_b(r)

    all_tiles = ker_tiles.at[pl.ds(0, 31)]
    pltpu.make_async_copy(all_tiles, all_tiles, ker_recv).wait()
    w_copies = []
    for r in (2, 1, 3):
        w_copies.append(remote(
            weights.at[y], weights.at[y], w_send.at[r - 1], w_recv.at[r - 1], along_y(r)
        ))
        w_copies[-1].start()

    fetch.wait()
    turn_by = (128 - (inch % 4) * 32) % 128

    def widen(k, carry):
        at = pl.ds(pl.multiple_of(k * 256, 256), 256)
        resp_wide[at, :] = pltpu.roll(resp_raw[at, :].astype(F32), turn_by, axis=1)
        return carry

    lax.fori_loop(0, 8, widen, 0)

    def merge(parts, bit):
        lane = lax.broadcasted_iota(jnp.int32, parts[0].shape, 1)
        high = (lane & (8 * bit)) != 0
        return [
            jnp.where(high, pltpu.roll(parts[i | bit], 8 * bit, axis=1), parts[i])
            for i in range(len(parts)) if not i & bit
        ]

    def pack_response(b, carry):
        for half in range(2):
            parts = [
                resp_wide[pl.ds(b * 32 + half * 16 + p, 8, stride=256), :] for p in range(16)
            ]
            parts = merge(merge(parts, 8), 4)
            parts = swap_stage(swap_stage(parts, 1), 2)
            for g in range(4):
                resp_out[g, b, :, half * 128:(half + 1) * 128] = parts[g]
        return carry

    lax.fori_loop(0, 8, pack_response, 0)
    rows_s = pl.ds(pl.multiple_of(s * 8, 8), 8)
    resp_copies = []
    for r in (1, 2, 3):
        resp_copies.append(remote(
            resp_out.at[(s + r) % 4], response.at[:, rows_s, :],
            resp_send.at[r - 1], resp_recv.at[r - 1], in_group(r),
        ))
        resp_copies[-1].start()
    response[:, rows_s, :] = resp_out[s]

    ca_copies = []
    cb_copies = []
    for r in (0, 1, 3, 2):
        there = (x + 4 - r) % 4
        if r:
            xa_copies[place[r]].wait_recv()
        view = gathered.at[there // 2, core, there % 2, :, part_ha]
        ca_copies.append(remote(view, view, ca_send.at[r], ca_recv.at[r], other))
        ca_copies[-1].start()
        for k in (1, 2, 3):
            zb_copies[r, k].wait_recv()
        view = gathered.at[there // 2, core, there % 2, :, part_b]
        cb_copies.append(remote(view, view, cb_send.at[r], cb_recv.at[r], other))
        cb_copies[-1].start()

    def upright(hi, of_core):
        def one(k, carry):
            lanes = pl.ds(pl.multiple_of(256 + k * 128, 128), 128)
            block = jnp.concatenate(
                [gathered[hi, of_core, 0, :, lanes], gathered[hi, of_core, 1, :, lanes]], axis=0
            )
            at = pl.multiple_of(256 + (hi * 2 + of_core) * 2048 + k * 128, 128)
            rows[pl.ds(at, 128), :] = block.astype(F32).T
            return carry

        lax.fori_loop(0, 16, one, 0)

    for hi in range(2):
        upright(hi, core)
    for copy in ca_copies + cb_copies:
        copy.wait_recv()
    for hi in range(2):
        upright(hi, 1 - core)
    at_start = y == 0
    for k in range(2):
        block = jnp.concatenate(
            [gathered[0, 0, lo, :, k * 128:(k + 1) * 128] for lo in range(2)], axis=0
        )
        rows[k * 128:(k + 1) * 128, :] = jnp.where(at_start, 0.0, block.astype(F32).T)
    for q in range(8):
        xe[:, q * 128:(q + 1) * 128] = rows[(7 - q) * 32:(8 - q) * 32, :].astype(BF16)

    def order(p, carry):
        for b in range(8):
            sb[p, b * 32:(b + 1) * 32, :] = rows[
                pl.ds(b * 32 + p, 32, stride=256), :
            ].astype(BF16)
            sb[p, 256 + b * 32:256 + (b + 1) * 32, :] = rows[
                pl.ds(256 + b * 32 + p, 32, stride=256), :
            ].astype(BF16)
        return carry

    lax.fori_loop(0, 32, order, 0)

    for copy in w_copies + resp_copies:
        copy.wait()

    wide_lane = lax.broadcasted_iota(jnp.int32, (256, 256), 1)
    wide_row = lax.broadcasted_iota(jnp.int32, (256, 256), 0)
    ext_lane = lax.broadcasted_iota(jnp.int32, (32, 256), 1)
    ext_row = lax.broadcasted_iota(jnp.int32, (32, 256), 0)

    def forward(taps):
        def tap_matrix():
            return jnp.concatenate([taps[j] for j in range(4)], axis=0)

        acc[...] = jnp.zeros_like(acc)

        def group(g, carry):
            lhs = jnp.concatenate(
                [
                    jnp.concatenate(
                        [sb[g * 4 + j, (8 - q) * 32:(8 - q) * 32 + 256, :] for q in range(8)],
                        axis=1,
                    )
                    for j in range(4)
                ],
                axis=0,
            )
            product = jnp.dot(lhs, tap_matrix(), preferred_element_type=F32)
            here = acc[0:256, :]
            after = acc[256:512, :]
            for j in range(4):
                shift = (g * 4 + j) * 8
                turned = pltpu.roll(product[j * 256:(j + 1) * 256], shift, axis=1)
                keep = wide_lane >= shift
                here = here + jnp.where(keep, turned, 0.0)
                after = after + jnp.where(keep, 0.0, turned)
            acc[0:256, :] = here
            acc[256:512, :] = after
            return carry

        lax.fori_loop(0, 8, group, 0)
        edge = jnp.dot(xe[...], tap_matrix(), preferred_element_type=F32)
        edge = pltpu.roll(edge, 0, axis=1, stride=8, stride_axis=0)
        edge = jnp.sum(jnp.where(ext_lane < ext_row * 8, edge, 0.0), axis=0, keepdims=True)
        after = acc[256:512, :]
        moved = jnp.where(
            wide_row >= 32, pltpu.roll(after, 32, axis=0), pltpu.roll(after, 33, axis=0)
        )
        moved = jnp.where(wide_row == 0, jnp.broadcast_to(edge, (256, 256)), moved)
        return (acc[0:256, :] + moved) * SCALE

    def expand(resid):
        later = jnp.where(
            wide_row < 224, pltpu.roll(resid, 224, axis=0), pltpu.roll(resid, 223, axis=0)
        )
        later = jnp.where(wide_row == 255, 0.0, later)
        here_t = resid.T
        later_t = later.T
        both = jnp.concatenate([here_t, later_t], axis=0)
        r_even[...] = both.astype(BF16)
        r_odd[...] = jnp.concatenate([both[8:], both[:8]], axis=0).astype(BF16)

    def edge_windows(resid):
        line = jnp.broadcast_to(resid[0:1, :], (32, 256))
        line = pltpu.roll(line, 8, axis=1, stride=8, stride_axis=0)
        return jnp.where(ext_lane + (31 - ext_row) * 8 >= 256, line, 0.0)

    def gradient_of(there, edges):
        total = jnp.zeros((256, 256), F32)
        top = pl.multiple_of((8 - 2 * there) * 32, 32)
        low = pl.multiple_of((7 - 2 * there) * 32, 32)
        for g in range(8):
            left = []
            right = []
            for p in range(4 * g, 4 * g + 4):
                windows = r_odd if p % 2 else r_even
                at = 8 * (p - p % 2)
                left.append(windows[at:at + 256, :])
                right.append(jnp.concatenate(
                    [sb[p, pl.ds(top, 256), :], sb[p, pl.ds(low, 256), :]], axis=1
                ))
            total = total + jnp.dot(
                jnp.concatenate(left, axis=1), jnp.concatenate(right, axis=0),
                preferred_element_type=F32,
            )
        lanes = pl.ds(pl.multiple_of(there * 256, 256), 256)
        total = total + jnp.dot(edges, xe[:, lanes], preferred_element_type=F32)
        return total.T * SCALE

    def send_energy(turn):
        energy_own[turn, 0] = jnp.full((8, 128), jnp.sum(grad_own[...] * grad_own[...]), F32)

        def send(r, carry):
            remote(
                energy_own.at[turn, 0], energy_a.at[turn, r - 1],
                ea_send.at[turn], ea_recv.at[turn], in_plane((rank + r) % 32),
            ).start()
            return carry

        lax.fori_loop(1, 32, send, 0)

    def send_tiles(turn):

        def send(r, carry):
            d = (rank + r) % 32
            to = d // 4
            rows_d = pl.multiple_of(((d % 4) // 2) * 128 + (to % 2) * 64 + (to // 2) * 16, 16)
            lanes = pl.ds(pl.multiple_of((d % 2) * 128, 128), 128)
            remote(
                grad_all.at[turn, y, pl.ds(rows_d, 16), lanes], tiles.at[turn, rank],
                t_send.at[turn], t_recv.at[turn], in_plane(d),
            ).start()
            return carry

        lax.fori_loop(1, 32, send, 0)
        tiles[turn, rank] = grad_all[turn, y, pl.ds(row_k, 16), pl.ds(lane_k, 128)]

    def pass_energy(turn):
        mine = energy_a.at[turn]
        pltpu.make_async_copy(mine, mine, ea_recv.at[turn]).wait()
        energy_own[turn, 1] = energy_own[turn, 0] + jnp.sum(energy_a[turn], axis=0)
        copies = []
        for r in (1, 2, 3):
            copies.append(remote(
                energy_own.at[turn, 1], energy_b.at[turn, r - 1],
                eb_send.at[turn, r - 1], eb_recv.at[turn, r - 1], along_y(r),
            ))
            copies[-1].start()
        return copies

    def finish_energy(turn, copies):
        for copy in copies:
            copy.wait()
        total = energy_own[turn, 1] + jnp.sum(energy_b[turn], axis=0)
        factor = STEP_SIZE * lax.rsqrt(total / COUNT + EPSILON)
        return factor[0:1, :]

    factors = []
    resid_copies = []
    energy_copies = None
    for turn in range(2):
        if turn == 0:
            predicted = forward(weights)
            base[...] = predicted
        else:
            change = forward(grad_all.at[0])
            factors.append(finish_energy(0, energy_copies))
            wide = jnp.concatenate([factors[0], factors[0]], axis=1)
            predicted = base[...] + wide * change
        resid = (response[...].reshape(256, 256) - predicted).astype(BF16).astype(F32)
        if turn == 1:
            resid_all[...] = resid.reshape(8, 32, 256)
            for r in (1, 2, 3):
                there = pl.ds(pl.multiple_of(((s + r) % 4) * 8, 8), 8)
                resid_copies.append(remote(
                    resid_all.at[:, there, :], resid_in.at[s],
                    o_send.at[r - 1], o_recv.at[r - 1], in_group(r),
                ))
                resid_copies[-1].start()
            resid_in[s] = resid_all[:, rows_s, :]
        expand(resid)
        flipped = edge_windows(resid)
        edges = jnp.concatenate(
            [flipped[31 - j:32 - j, :] for j in range(32)], axis=0
        ).T.astype(BF16)
        rs_copies = []
        for r in (2, 1, 3):
            grad_out[r - 1] = gradient_of((y + r) % 4, edges).astype(BF16)
            rs_copies.append(remote(
                grad_out.at[r - 1], grad_in.at[r - 1],
                rs_send.at[turn, r - 1], rs_recv.at[turn, r - 1], along_y(r),
            ))
            rs_copies[-1].start()
        own = gradient_of(y, edges)
        for copy in rs_copies:
            copy.wait()
        for r in range(3):
            own = own + grad_in[r].astype(F32)
        grad_own[...] = own
        grad_all[turn, y] = own.astype(BF16)
        ag_copies = []
        if turn == 0:
            for r in (2, 1, 3):
                ag_copies.append(remote(
                    grad_all.at[turn, y], grad_all.at[turn, y],
                    ag_send.at[r - 1], ag_recv.at[r - 1], along_y(r),
                ))
                ag_copies[-1].start()
        send_energy(turn)
        send_tiles(turn)
        energy_copies = pass_energy(turn)
        for copy in ag_copies:
            copy.wait()

    for copy in resid_copies:
        copy.wait()

    def unpack_residual(b, carry):
        for half in range(2):
            parts = [resid_in[g, b, :, half * 128:(half + 1) * 128] for g in range(4)]
            parts = swap_stage(swap_stage(parts, 1), 2)
            for m in range(4):
                for l in range(4):
                    part = parts[l] if m == 0 else pltpu.roll(parts[l], 128 - 32 * m, axis=1)
                    at = b * 32 + half * 16 + 4 * m + l
                    resid_wide[pl.ds(at, 8, stride=256), :] = part
        return carry

    lax.fori_loop(0, 8, unpack_residual, 0)
    for k in range(16):
        flat = resid_wide[k * 128:(k + 1) * 128, :].T
        resid_ref[:, k * 128:(k + 1) * 128] = flat[0:32, :].astype(BF16)

    factors.append(finish_energy(1, energy_copies))
    for turn in range(2):
        half = tiles.at[turn, pl.ds(0, 31)]
        pltpu.make_async_copy(half, half, t_recv.at[turn]).wait()
    for half in range(2):
        steps = [
            factors[0] * tiles[0, half * 16 + d].astype(F32)
            + factors[1] * tiles[1, half * 16 + d].astype(F32)
            for d in range(16)
        ]
        lanes = slice(half * 128, (half + 1) * 128)
        for u, step in enumerate(swap_blocks(steps)):
            kernel_ref[u, :, lanes] = ker_ref[u, :, lanes] + step

    pltpu.make_async_copy(all_tiles, all_tiles, ker_send).wait()
    for copy in za_copies + zh_copies + xb_copies + xa_copies + ca_copies + cb_copies:
        copy.wait_send()
    for copy in zb_copies.values():
        copy.wait_send()
    for turn in range(2):
        mine = energy_a.at[turn]
        pltpu.make_async_copy(mine, mine, ea_send.at[turn]).wait()
        half = tiles.at[turn, pl.ds(0, 31)]
        pltpu.make_async_copy(half, half, t_send.at[turn]).wait()


def local(signal, response, kernel):
    dma = pltpu.SemaphoreType.DMA
    vmem = pl.BlockSpec(memory_space=pltpu.VMEM)
    kernel_out, resid = pl.pallas_call(
        body,
        out_shape=(
            jax.ShapeDtypeStruct((16, 16, 256), F32),
            jax.ShapeDtypeStruct((32, 2048), BF16),
        ),
        in_specs=[vmem, pl.BlockSpec(memory_space=pl.ANY), vmem],
        out_specs=(vmem, vmem),
        scratch_shapes=[
            pltpu.VMEM((2, 2, 2, 64, 2304), BF16),
            pltpu.VMEM((8448, 128), F32),
            pltpu.VMEM((32, 16, 128), BF16),
            pltpu.VMEM((2048, 128), BF16),
            pltpu.VMEM((2048, 128), F32),
            pltpu.VMEM((4, 8, 8, 256), F32),
            pltpu.VMEM((2048, 128), F32),
            pltpu.VMEM((256, 256), F32),
            pltpu.VMEM((32, 512, 128), BF16),
            pltpu.VMEM((32, 1024), BF16),
            pltpu.VMEM((4, 256, 256), BF16),
            pltpu.VMEM((8, 32, 256), F32),
            pltpu.VMEM((512, 256), BF16),
            pltpu.VMEM((512, 256), BF16),
            pltpu.VMEM((3, 256, 256), BF16),
            pltpu.VMEM((3, 256, 256), BF16),
            pltpu.VMEM((256, 256), F32),
            pltpu.VMEM((2, 4, 256, 256), BF16),
            pltpu.VMEM((2, 32, 16, 128), BF16),
            pltpu.VMEM((2, 31, 8, 128), F32),
            pltpu.VMEM((2, 3, 8, 128), F32),
            pltpu.VMEM((2, 2, 8, 128), F32),
            pltpu.VMEM((512, 256), F32),
            pltpu.VMEM((8, 32, 256), F32),
            pltpu.VMEM((4, 8, 8, 256), F32),
            dma, dma, dma, dma((3,)), dma((3,)), dma, dma,
            dma((3,)), dma((3,)), dma((3,)), dma((3,)), dma((3,)), dma((3,)), dma((3,)), dma((3,)),
            dma((4, 3)), dma((4, 3)), dma((4,)), dma((4,)), dma((4,)), dma((4,)),
            dma((3,)), dma((3,)), dma((2, 3)), dma((2, 3)), dma((3,)), dma((3,)),
            dma((2,)), dma((2,)), dma((2, 3)), dma((2, 3)), dma((2,)), dma((2,)), dma((3,)), dma((3,)),
        ],
        compiler_params=pltpu.CompilerParams(
            collective_id=0, has_side_effects=True, vmem_limit_bytes=60 * 2**20
        ),
    )(signal.T, response, kernel)
    return kernel_out, resid.T


def solution(mesh):
    placed = (P("tm", "inch"), P("tm", None), P("tm", "inch", None))
    return jax.shard_map(
        local,
        mesh=mesh,
        in_specs=placed,
        out_specs=(P("tm", "inch", None), P("tm", "inch")),
        check_vma=False,
    )
```

```python
import math

import jax
import jax.numpy as jnp
from jax import lax
from jax.experimental import pallas as pl
from jax.experimental.pallas import tpu as pltpu
from jax.sharding import PartitionSpec as P

STEP_SIZE = 0.5
EPSILON = 1e-06
F32 = jnp.float32
BF16 = jnp.bfloat16
MESH = pl.DeviceIdType.MESH
TAPS = 256
CI = 128
CO = 256
SCALE = 1.0 / math.sqrt(TAPS * CI)
COUNT = TAPS * CI * CO


def remote(src, dst, send, recv, device):
    return pltpu.make_async_remote_copy(
        src_ref=src, dst_ref=dst, send_sem=send, recv_sem=recv,
        device_id=device, device_id_type=MESH,
    )


def swap_blocks(parts):
    parts = list(parts)
    for bit in (1, 2, 4, 8):
        parts = swap_stage(parts, bit)
    return parts


def swap_stage(parts, bit):
    lane = lax.broadcasted_iota(jnp.int32, parts[0].shape, 1)
    high = (lane & (8 * bit)) != 0
    result = list(parts)
    for i in range(len(parts)):
        if not i & bit:
            low_part, high_part = parts[i], parts[i | bit]
            result[i] = jnp.where(high, pltpu.roll(high_part, 8 * bit, axis=1), low_part)
            result[i | bit] = jnp.where(
                high, high_part, pltpu.roll(low_part, 128 - 8 * bit, axis=1)
            )
    return result


def body(
    sig_ref, resp_hbm, ker_ref,
    kernel_ref, resid_ref,
    gathered, rows, halo, ker_tiles, resp_raw, resp_wide, resp_out, resid_wide, base,
    sb, xe, taps, response, r_even, r_odd,
    grad_out, grad_in, grad_own, tiles, factor_rows, energy_a, energy_b, energy_own, acc, resid_all,
    resid_in, edge_t,
    hbm_sem, ker_send, ker_recv, resp_send, resp_recv, tail_send, tail_recv,
    za_send, za_recv, zh_send, zh_recv, xb_send, xb_recv, xa_send, xa_recv,
    zb_send, zb_recv, ca_send, ca_recv, cb_send, cb_recv,
    w_send, w_recv, rs_send, rs_recv, ag_send, ag_recv,
    ea_send, ea_recv, eb_send, eb_recv, t_send, t_recv, o_send, o_recv,
):
    tm = lax.axis_index("tm")
    inch = lax.axis_index("inch")
    y = tm // 4
    s = tm % 4
    x_hi = s // 2
    core = s % 2
    z = inch // 2
    x_lo = inch % 2
    x = x_hi * 2 + x_lo
    rank = inch * 4 + s

    def in_plane(d):
        return (y * 4 + d % 4, d // 4)

    def along_y(r):
        return ((((y + r) % 4) * 4) + s, inch)

    def along_z(r):
        return (tm, ((z + r) % 4) * 2 + x_lo)

    def along_x(r):
        there = (x + r) % 4
        return (y * 4 + (there // 2) * 2 + core, z * 2 + there % 2)

    def in_group(r):
        return (y * 4 + (s + r) % 4, inch)

    barrier = pltpu.get_barrier_semaphore()

    def greet(r, carry):
        pl.semaphore_signal(
            barrier, inc=1, device_id=in_plane((rank + r) % 32), device_id_type=MESH
        )
        return carry

    lax.fori_loop(1, 32, greet, 0)
    for r in (1, 2, 3):
        pl.semaphore_signal(barrier, inc=1, device_id=along_y(r), device_id_type=MESH)
    pl.semaphore_signal(
        barrier, inc=1, device_id=((tm + 15) % 16, inch), device_id_type=MESH
    )

    columns = pl.ds(pl.multiple_of((inch // 4) * 128, 128), 128)
    fetch = pltpu.make_async_copy(resp_hbm.at[:, columns], resp_raw, hbm_sem)
    fetch.start()
    row_z = pl.ds(pl.multiple_of(z * 16, 16), 16)
    lane16 = lax.broadcasted_iota(jnp.int32, (16, 128), 1)
    parts = [sig_ref[:, k * 128:(k + 1) * 128].astype(F32) for k in range(16)]
    for bit in (1, 2, 4):
        high = (lane16 & bit) != 0
        for i in range(16):
            if not i & (2 * bit):
                one, two = parts[i], parts[i | (2 * bit)]
                parts[i] = jnp.where(high, pltpu.roll(two, bit, axis=1), one)
                parts[i | (2 * bit)] = jnp.where(high, two, pltpu.roll(one, 128 - bit, axis=1))
    for k in range(16):
        gathered[x_hi, core, x_lo, row_z, 256 + k * 128:384 + k * 128] = parts[k].astype(BF16)
    part_h, part_a, part_b = pl.ds(0, 256), pl.ds(256, 1024), pl.ds(1280, 1024)
    part_ha = pl.ds(0, 1280)

    pl.semaphore_wait(barrier, 35)

    nxt = (tm + 1) % 16
    tail_copy = remote(
        sig_ref.at[:, pl.ds(1792, 256)],
        gathered.at[(nxt % 4) // 2, nxt % 2, x_lo, row_z, part_h],
        tail_send, tail_recv, (nxt, inch),
    )
    tail_copy.start()
    za_copies = []
    xb_copies = []
    for r in (2, 1, 3):
        view = gathered.at[x_hi, core, x_lo, row_z, part_a]
        za_copies.append(remote(view, view, za_send.at[r - 1], za_recv.at[r - 1], along_z(r)))
        za_copies[-1].start()
        view = gathered.at[x_hi, core, x_lo, row_z, part_b]
        xb_copies.append(remote(view, view, xb_send.at[r - 1], xb_recv.at[r - 1], along_x(r)))
        xb_copies[-1].start()

    for half in range(2):
        swapped = swap_blocks([ker_ref[u, :, half * 128:(half + 1) * 128] for u in range(16)])
        for d in range(16):
            ker_tiles[half * 16 + d] = swapped[d].astype(BF16)
    row_k = pl.multiple_of((s // 2) * 128 + x_lo * 64 + z * 16, 16)
    lane_k = pl.multiple_of((s % 2) * 128, 128)

    def send_taps(r, carry):
        d = (rank + r) % 32
        remote(
            ker_tiles.at[d], taps.at[0, y, pl.ds(row_k, 16), pl.ds(lane_k, 128)],
            ker_send, ker_recv, in_plane(d),
        ).start()
        return carry

    lax.fori_loop(1, 32, send_taps, 0)
    taps[0, y, pl.ds(row_k, 16), pl.ds(lane_k, 128)] = ker_tiles[rank]

    tail_copy.wait()
    zh_copies = []
    for r in (2, 1, 3):
        view = gathered.at[x_hi, core, x_lo, row_z, part_h]
        zh_copies.append(remote(view, view, zh_send.at[r - 1], zh_recv.at[r - 1], along_z(r)))
        zh_copies[-1].start()

    other = (y * 4 + x_hi * 2 + 1 - core, inch)
    zb_copies = {}

    def pass_b(r):
        there = (x + 4 - r) % 4
        for k in (2, 1, 3):
            view = gathered.at[there // 2, core, there % 2, row_z, part_b]
            copy = remote(view, view, zb_send.at[r, k - 1], zb_recv.at[r, k - 1], along_z(k))
            copy.start()
            zb_copies[r, k] = copy

    place = {2: 0, 1: 1, 3: 2}
    pass_b(0)
    for copy in za_copies + zh_copies:
        copy.wait_recv()
    xa_copies = []
    for r in (2, 1, 3):
        view = gathered.at[x_hi, core, x_lo, :, part_ha]
        xa_copies.append(remote(view, view, xa_send.at[r - 1], xa_recv.at[r - 1], along_x(r)))
        xa_copies[-1].start()
    for r in (1, 3, 2):
        xb_copies[place[r]].wait_recv()
        pass_b(r)

    all_tiles = ker_tiles.at[pl.ds(0, 31)]
    pltpu.make_async_copy(all_tiles, all_tiles, ker_recv).wait()
    w_copies = []
    for r in (2, 1, 3):
        w_copies.append(remote(
            taps.at[0, y], taps.at[0, y], w_send.at[r - 1], w_recv.at[r - 1], along_y(r)
        ))
        w_copies[-1].start()

    fetch.wait()
    turn_by = (128 - (inch % 4) * 32) % 128

    def widen(k, carry):
        at = pl.ds(pl.multiple_of(k * 256, 256), 256)
        resp_wide[at, :] = pltpu.roll(resp_raw[at, :].astype(F32), turn_by, axis=1)
        return carry

    lax.fori_loop(0, 8, widen, 0)

    def merge(parts, bit):
        lane = lax.broadcasted_iota(jnp.int32, parts[0].shape, 1)
        high = (lane & (8 * bit)) != 0
        return [
            jnp.where(high, pltpu.roll(parts[i | bit], 8 * bit, axis=1), parts[i])
            for i in range(len(parts)) if not i & bit
        ]

    def pack_response(b, carry):
        for half in range(2):
            parts = [
                resp_wide[pl.ds(b * 32 + half * 16 + p, 8, stride=256), :] for p in range(16)
            ]
            parts = merge(merge(parts, 8), 4)
            parts = swap_stage(swap_stage(parts, 1), 2)
            for g in range(4):
                resp_out[g, b, :, half * 128:(half + 1) * 128] = parts[g]
        return carry

    lax.fori_loop(0, 8, pack_response, 0)
    rows_s = pl.ds(pl.multiple_of(s * 8, 8), 8)
    resp_copies = []
    for r in (1, 2, 3):
        resp_copies.append(remote(
            resp_out.at[(s + r) % 4], response.at[:, rows_s, :],
            resp_send.at[r - 1], resp_recv.at[r - 1], in_group(r),
        ))
        resp_copies[-1].start()
    response[:, rows_s, :] = resp_out[s]

    ca_copies = []
    cb_copies = []
    for r in (0, 1, 3, 2):
        there = (x + 4 - r) % 4
        if r:
            xa_copies[place[r]].wait_recv()
        view = gathered.at[there // 2, core, there % 2, :, part_ha]
        ca_copies.append(remote(view, view, ca_send.at[r], ca_recv.at[r], other))
        ca_copies[-1].start()
        for k in (1, 2, 3):
            zb_copies[r, k].wait_recv()
        view = gathered.at[there // 2, core, there % 2, :, part_b]
        cb_copies.append(remote(view, view, cb_send.at[r], cb_recv.at[r], other))
        cb_copies[-1].start()

    def upright(hi, of_core):
        def one(k, carry):
            for m in range(8):
                lanes = pl.ds(pl.multiple_of(256 + (k * 8 + m) * 128, 128), 128)
                block = jnp.concatenate(
                    [gathered[hi, of_core, 0, :, lanes], gathered[hi, of_core, 1, :, lanes]], axis=0
                )
                rows[hi * 2 + of_core, k * 8 + m] = block.T.astype(F32)
            return carry

        lax.fori_loop(0, 2, one, 0)

    for hi in range(2):
        upright(hi, core)
    for copy in ca_copies + cb_copies:
        copy.wait_recv()
    for hi in range(2):
        upright(hi, 1 - core)
    at_start = y == 0
    for k in range(2):
        block = jnp.concatenate(
            [gathered[0, 0, lo, :, k * 128:(k + 1) * 128] for lo in range(2)], axis=0
        )
        halo[k * 128:(k + 1) * 128, :] = jnp.where(at_start, 0.0, block.astype(F32).T)
    for q in range(8):
        xe[:, q * 128:(q + 1) * 128] = halo[(7 - q) * 32:(8 - q) * 32, :].astype(BF16)
    first = lax.broadcasted_iota(jnp.int32, (32, 128), 0) == 0

    def order(p, carry):
        for b in range(8):
            at = pl.multiple_of((b % 4) * 32 + (p // 8) * 8, 8)
            block = jnp.concatenate(
                [rows[g, (p % 8) * 2 + b // 4, pl.ds(at, 8), :] for g in range(4)], axis=0
            )
            edge = jnp.broadcast_to(halo[pl.ds(b * 32 + p, 1), :], (32, 128))
            before = jnp.where(first, edge, pltpu.roll(block, 1, axis=0))
            sb[p, b * 32:(b + 1) * 32, :] = before.astype(BF16)
            sb[p, 256 + b * 32:256 + (b + 1) * 32, :] = block.astype(BF16)
        return carry

    lax.fori_loop(0, 32, order, 0)

    for copy in w_copies + resp_copies:
        copy.wait()

    wide_lane = lax.broadcasted_iota(jnp.int32, (256, 256), 1)
    wide_row = lax.broadcasted_iota(jnp.int32, (256, 256), 0)
    ext_lane = lax.broadcasted_iota(jnp.int32, (32, 256), 1)
    ext_row = lax.broadcasted_iota(jnp.int32, (32, 256), 0)

    def forward(turn):
        def tap_matrix():
            return jnp.concatenate([taps[turn, j] for j in range(4)], axis=0)

        acc[...] = jnp.zeros_like(acc)

        def group(g, carry):
            lhs = jnp.concatenate(
                [
                    jnp.concatenate(
                        [sb[g * 4 + j, (8 - q) * 32:(8 - q) * 32 + 256, :] for q in range(8)],
                        axis=1,
                    )
                    for j in range(4)
                ],
                axis=0,
            )
            product = jnp.dot(lhs, tap_matrix(), preferred_element_type=F32)
            here = acc[0:256, :]
            after = acc[256:512, :]
            for j in range(4):
                shift = (g * 4 + j) * 8
                turned = pltpu.roll(product[j * 256:(j + 1) * 256], shift, axis=1)
                keep = wide_lane >= shift
                here = here + jnp.where(keep, turned, 0.0)
                after = after + jnp.where(keep, 0.0, turned)
            acc[0:256, :] = here
            acc[256:512, :] = after
            return carry

        lax.fori_loop(0, 8, group, 0)
        edge = jnp.dot(xe[...], tap_matrix(), preferred_element_type=F32)
        edge = pltpu.roll(edge, 0, axis=1, stride=8, stride_axis=0)
        edge = jnp.sum(jnp.where(ext_lane < ext_row * 8, edge, 0.0), axis=0, keepdims=True)
        after = acc[256:512, :]
        moved = jnp.where(
            wide_row >= 32, pltpu.roll(after, 32, axis=0), pltpu.roll(after, 33, axis=0)
        )
        moved = jnp.where(wide_row == 0, jnp.broadcast_to(edge, (256, 256)), moved)
        return (acc[0:256, :] + moved) * SCALE

    def expand(resid):
        later = jnp.where(
            wide_row < 224, pltpu.roll(resid, 224, axis=0), pltpu.roll(resid, 223, axis=0)
        )
        later = jnp.where(wide_row == 255, 0.0, later)
        here_t = resid.T
        later_t = later.T
        both = jnp.concatenate([here_t, later_t], axis=0)
        r_even[...] = both.astype(BF16)
        r_odd[...] = jnp.concatenate([both[8:], both[:8]], axis=0).astype(BF16)

    def edge_windows(resid):
        line = jnp.broadcast_to(resid[0:1, :], (32, 256))
        line = pltpu.roll(line, 8, axis=1, stride=8, stride_axis=0)
        return jnp.where(ext_lane + (31 - ext_row) * 8 >= 256, line, 0.0)

    def gradient_of(there, edges):
        total = jnp.zeros((256, 256), F32)
        top = pl.multiple_of((8 - 2 * there) * 32, 32)
        low = pl.multiple_of((7 - 2 * there) * 32, 32)
        for g in range(8):
            left = []
            right = []
            for p in range(4 * g, 4 * g + 4):
                windows = r_odd if p % 2 else r_even
                at = 8 * (p - p % 2)
                left.append(windows[at:at + 256, :])
                right.append(jnp.concatenate(
                    [sb[p, pl.ds(top, 256), :], sb[p, pl.ds(low, 256), :]], axis=1
                ))
            total = total + jnp.dot(
                jnp.concatenate(left, axis=1), jnp.concatenate(right, axis=0),
                preferred_element_type=F32,
            )
        lanes = pl.ds(pl.multiple_of(there * 256, 256), 256)
        total = total + jnp.dot(edges, xe[:, lanes], preferred_element_type=F32)
        return total.T * SCALE

    def send_energy(turn):
        energy_own[turn, 0] = jnp.full((8, 128), jnp.sum(grad_own[...] * grad_own[...]), F32)

        def send(r, carry):
            remote(
                energy_own.at[turn, 0], energy_a.at[turn, r - 1],
                ea_send.at[turn], ea_recv.at[turn], in_plane((rank + r) % 32),
            ).start()
            return carry

        lax.fori_loop(1, 32, send, 0)

    def send_tiles(turn):

        def send(r, carry):
            d = (rank + r) % 32
            to = d // 4
            rows_d = pl.multiple_of(((d % 4) // 2) * 128 + (to % 2) * 64 + (to // 2) * 16, 16)
            lanes = pl.ds(pl.multiple_of((d % 2) * 128, 128), 128)
            remote(
                taps.at[turn + 1, y, pl.ds(rows_d, 16), lanes], tiles.at[turn, rank],
                t_send.at[turn], t_recv.at[turn], in_plane(d),
            ).start()
            return carry

        lax.fori_loop(1, 32, send, 0)
        tiles[turn, rank] = taps[turn + 1, y, pl.ds(row_k, 16), pl.ds(lane_k, 128)]

    def energy_copy(turn, r):
        return remote(
            energy_own.at[turn, 1], energy_b.at[turn, r - 1],
            eb_send.at[turn, r - 1], eb_recv.at[turn, r - 1], along_y(r),
        )

    def pass_energy(turn):
        mine = energy_a.at[turn]
        pltpu.make_async_copy(mine, mine, ea_recv.at[turn]).wait()
        energy_own[turn, 1] = energy_own[turn, 0] + jnp.sum(energy_a[turn], axis=0)
        for r in (1, 2, 3):
            energy_copy(turn, r).start()

    def finish_energy(turn):
        for r in (1, 2, 3):
            energy_copy(turn, r).wait()
        total = energy_own[turn, 1] + jnp.sum(energy_b[turn], axis=0)
        factor_rows[turn + 1] = STEP_SIZE * lax.rsqrt(total / COUNT + EPSILON)

    def resid_copy(r):
        there = pl.ds(pl.multiple_of(((s + r) % 4) * 8, 8), 8)
        return remote(
            resid_all.at[:, there, :], resid_in.at[s],
            o_send.at[r - 1], o_recv.at[r - 1], in_group(r),
        )

    def shard_copy(turn, r):
        return remote(
            grad_out.at[r - 1], grad_in.at[r - 1],
            rs_send.at[turn, r - 1], rs_recv.at[turn, r - 1], along_y(r),
        )

    def gather_copy(r):
        return remote(
            taps.at[1, y], taps.at[1, y], ag_send.at[r - 1], ag_recv.at[r - 1], along_y(r)
        )

    base[...] = jnp.zeros_like(base)
    factor_rows[0] = jnp.ones((8, 128), F32)

    def iterate(turn, carry):
        change = forward(turn)

        @pl.when(turn == 1)
        def _():
            finish_energy(0)

        factor = factor_rows[turn, 0:1, :]
        predicted = base[...] + jnp.concatenate([factor, factor], axis=1) * change
        base[...] = predicted
        resid = (response[...].reshape(256, 256) - predicted).astype(BF16).astype(F32)

        @pl.when(turn == 1)
        def _():
            resid_all[...] = resid.reshape(8, 32, 256)
            for r in (1, 2, 3):
                resid_copy(r).start()
            resid_in[s] = resid_all[:, rows_s, :]

        expand(resid)
        flipped = edge_windows(resid)
        edge_t[...] = jnp.concatenate(
            [flipped[31 - j:32 - j, :] for j in range(32)], axis=0
        ).T.astype(BF16)

        def chunk(j, carry):
            up = (6 - j) % 4
            late = j // 2
            r = up * (1 - late) + (3 - up) * late
            part = gradient_of((y + r) % 4, edge_t[...])

            @pl.when(j < 3)
            def _():
                grad_out[r - 1] = part.astype(BF16)
                shard_copy(turn, r).start()

            @pl.when(j == 3)
            def _():
                grad_own[...] = part

            return carry

        lax.fori_loop(0, 4, chunk, 0)
        for r in (1, 3, 2):
            shard_copy(turn, r).wait()
        own = grad_own[...]
        for r in range(3):
            own = own + grad_in[r].astype(F32)
        grad_own[...] = own
        taps[turn + 1, y] = own.astype(BF16)

        @pl.when(turn == 0)
        def _():
            for r in (2, 1, 3):
                gather_copy(r).start()

        send_energy(turn)
        send_tiles(turn)
        pass_energy(turn)

        @pl.when(turn == 0)
        def _():
            for r in (1, 3, 2):
                gather_copy(r).wait()

        return carry

    lax.fori_loop(0, 2, iterate, 0)

    for r in (1, 2, 3):
        resid_copy(r).wait()

    def unpack_residual(b, carry):
        for half in range(2):
            parts = [resid_in[g, b, :, half * 128:(half + 1) * 128] for g in range(4)]
            parts = swap_stage(swap_stage(parts, 1), 2)
            for m in range(4):
                for l in range(4):
                    part = parts[l] if m == 0 else pltpu.roll(parts[l], 128 - 32 * m, axis=1)
                    at = b * 32 + half * 16 + 4 * m + l
                    resid_wide[pl.ds(at, 8, stride=256), :] = part
        return carry

    lax.fori_loop(0, 8, unpack_residual, 0)
    for k in range(16):
        flat = resid_wide[k * 128:(k + 1) * 128, :].T
        resid_ref[:, k * 128:(k + 1) * 128] = flat[0:32, :].astype(BF16)

    finish_energy(1)
    factors = [factor_rows[1, 0:1, :], factor_rows[2, 0:1, :]]
    for turn in range(2):
        half = tiles.at[turn, pl.ds(0, 31)]
        pltpu.make_async_copy(half, half, t_recv.at[turn]).wait()
    for half in range(2):
        steps = [
            factors[0] * tiles[0, half * 16 + d].astype(F32)
            + factors[1] * tiles[1, half * 16 + d].astype(F32)
            for d in range(16)
        ]
        lanes = slice(half * 128, (half + 1) * 128)
        for u, step in enumerate(swap_blocks(steps)):
            kernel_ref[u, :, lanes] = ker_ref[u, :, lanes] + step

    pltpu.make_async_copy(all_tiles, all_tiles, ker_send).wait()
    for copy in za_copies + zh_copies + xb_copies + xa_copies + ca_copies + cb_copies:
        copy.wait_send()
    for copy in zb_copies.values():
        copy.wait_send()
    for turn in range(2):
        mine = energy_a.at[turn]
        pltpu.make_async_copy(mine, mine, ea_send.at[turn]).wait()
        half = tiles.at[turn, pl.ds(0, 31)]
        pltpu.make_async_copy(half, half, t_send.at[turn]).wait()


def local(signal, response, kernel):
    dma = pltpu.SemaphoreType.DMA
    vmem = pl.BlockSpec(memory_space=pltpu.VMEM)
    kernel_out, resid = pl.pallas_call(
        body,
        out_shape=(
            jax.ShapeDtypeStruct((16, 16, 256), F32),
            jax.ShapeDtypeStruct((32, 2048), BF16),
        ),
        in_specs=[vmem, pl.BlockSpec(memory_space=pl.ANY), vmem],
        out_specs=(vmem, vmem),
        scratch_shapes=[
            pltpu.VMEM((2, 2, 2, 64, 2304), BF16),
            pltpu.VMEM((4, 16, 128, 128), F32),
            pltpu.VMEM((256, 128), F32),
            pltpu.VMEM((32, 16, 128), BF16),
            pltpu.VMEM((2048, 128), BF16),
            pltpu.VMEM((2048, 128), F32),
            pltpu.VMEM((4, 8, 8, 256), F32),
            pltpu.VMEM((2048, 128), F32),
            pltpu.VMEM((256, 256), F32),
            pltpu.VMEM((32, 512, 128), BF16),
            pltpu.VMEM((32, 1024), BF16),
            pltpu.VMEM((3, 4, 256, 256), BF16),
            pltpu.VMEM((8, 32, 256), F32),
            pltpu.VMEM((512, 256), BF16),
            pltpu.VMEM((512, 256), BF16),
            pltpu.VMEM((3, 256, 256), BF16),
            pltpu.VMEM((3, 256, 256), BF16),
            pltpu.VMEM((256, 256), F32),
            pltpu.VMEM((2, 32, 16, 128), BF16),
            pltpu.VMEM((3, 8, 128), F32),
            pltpu.VMEM((2, 31, 8, 128), F32),
            pltpu.VMEM((2, 3, 8, 128), F32),
            pltpu.VMEM((2, 2, 8, 128), F32),
            pltpu.VMEM((512, 256), F32),
            pltpu.VMEM((8, 32, 256), F32),
            pltpu.VMEM((4, 8, 8, 256), F32),
            pltpu.VMEM((256, 32), BF16),
            dma, dma, dma, dma((3,)), dma((3,)), dma, dma,
            dma((3,)), dma((3,)), dma((3,)), dma((3,)), dma((3,)), dma((3,)), dma((3,)), dma((3,)),
            dma((4, 3)), dma((4, 3)), dma((4,)), dma((4,)), dma((4,)), dma((4,)),
            dma((3,)), dma((3,)), dma((2, 3)), dma((2, 3)), dma((3,)), dma((3,)),
            dma((2,)), dma((2,)), dma((2, 3)), dma((2, 3)), dma((2,)), dma((2,)), dma((3,)), dma((3,)),
        ],
        compiler_params=pltpu.CompilerParams(
            collective_id=0, has_side_effects=True, vmem_limit_bytes=60 * 2**20
        ),
    )(signal.T, response, kernel)
    return kernel_out, resid.T


def solution(mesh):
    placed = (P("tm", "inch"), P("tm", None), P("tm", "inch", None))
    return jax.shard_map(
        local,
        mesh=mesh,
        in_specs=placed,
        out_specs=(P("tm", "inch", None), P("tm", "inch")),
        check_vma=False,
    )
```

```python
import math

import jax
import jax.numpy as jnp
from jax import lax
from jax.experimental import pallas as pl
from jax.experimental.pallas import tpu as pltpu
from jax.sharding import PartitionSpec as P

STEP_SIZE = 0.5
EPSILON = 1e-06
F32 = jnp.float32
BF16 = jnp.bfloat16
MESH = pl.DeviceIdType.MESH
TAPS = 256
CI = 128
CO = 256
SCALE = 1.0 / math.sqrt(TAPS * CI)
COUNT = TAPS * CI * CO
WIDE = 16


def remote(src, dst, send, recv, device):
    return pltpu.make_async_remote_copy(
        src_ref=src, dst_ref=dst, send_sem=send, recv_sem=recv,
        device_id=device, device_id_type=MESH,
    )


def swap_blocks(parts):
    parts = list(parts)
    for bit in (1, 2, 4, 8):
        parts = swap_stage(parts, bit)
    return parts


def swap_stage(parts, bit):
    lane = lax.broadcasted_iota(jnp.int32, parts[0].shape, 1)
    high = (lane & (8 * bit)) != 0
    result = list(parts)
    for i in range(len(parts)):
        if not i & bit:
            low_part, high_part = parts[i], parts[i | bit]
            result[i] = jnp.where(high, pltpu.roll(high_part, 8 * bit, axis=1), low_part)
            result[i | bit] = jnp.where(
                high, high_part, pltpu.roll(low_part, 128 - 8 * bit, axis=1)
            )
    return result


def body(
    sig_ref, resp_hbm, ker_ref,
    kernel_ref, resid_ref,
    gathered, rows, halo, ker_tiles, resp_raw, resp_wide, resp_out, resid_wide, base,
    sb, xe, taps, response, r_even, r_odd,
    grad_out, grad_in, grad_own, tiles, factor_rows, energy_a, energy_b, energy_own, acc, resid_all,
    resid_in, edge_t,
    hbm_sem, ker_send, ker_recv, resp_send, resp_recv, tail_send, tail_recv,
    za_send, za_recv, zh_send, zh_recv, xb_send, xb_recv, xa_send, xa_recv,
    xh_send, xh_recv, ch_send, ch_recv, zb_send, zb_recv, ca_send, ca_recv, cb_send, cb_recv,
    w_send, w_recv, rs_send, rs_recv, ag_send, ag_recv,
    ea_send, ea_recv, eb_send, eb_recv, t_send, t_recv, o_send, o_recv,
):
    tm = lax.axis_index("tm")
    inch = lax.axis_index("inch")
    y = tm // 4
    s = tm % 4
    x_hi = s // 2
    core = s % 2
    z = inch // 2
    x_lo = inch % 2
    x = x_hi * 2 + x_lo
    rank = inch * 4 + s

    def in_plane(d):
        return (y * 4 + d % 4, d // 4)

    def along_y(r):
        return ((((y + r) % 4) * 4) + s, inch)

    def along_z(r):
        return (tm, ((z + r) % 4) * 2 + x_lo)

    def along_x(r):
        there = (x + r) % 4
        return (y * 4 + (there // 2) * 2 + core, z * 2 + there % 2)

    def in_group(r):
        return (y * 4 + (s + r) % 4, inch)

    barrier = pltpu.get_barrier_semaphore()

    def greet(r, carry):
        pl.semaphore_signal(
            barrier, inc=1, device_id=in_plane((rank + r) % 32), device_id_type=MESH
        )
        return carry

    lax.fori_loop(1, 32, greet, 0)
    for r in (1, 2, 3):
        pl.semaphore_signal(barrier, inc=1, device_id=along_y(r), device_id_type=MESH)

    columns = pl.ds(pl.multiple_of((inch // 4) * 128, 128), 128)
    fetch = pltpu.make_async_copy(resp_hbm.at[:, columns], resp_raw, hbm_sem)
    fetch.start()
    row_z = pl.ds(pl.multiple_of(z * 16, 16), 16)
    lane16 = lax.broadcasted_iota(jnp.int32, (16, 128), 1)
    parts = [sig_ref[:, k * 128:(k + 1) * 128].astype(F32) for k in range(16)]
    for bit in (1, 2, 4):
        high = (lane16 & bit) != 0
        for i in range(16):
            if not i & (2 * bit):
                one, two = parts[i], parts[i | (2 * bit)]
                parts[i] = jnp.where(high, pltpu.roll(two, bit, axis=1), one)
                parts[i | (2 * bit)] = jnp.where(high, two, pltpu.roll(one, 128 - bit, axis=1))
    for k in range(16):
        gathered[x_hi, core, x_lo, row_z, 256 + k * 128:384 + k * 128] = parts[k].astype(BF16)
    part_h, part_a, part_b = pl.ds(0, 256), pl.ds(256, 1024), pl.ds(1280, 1024)

    pl.semaphore_wait(barrier, 34)

    own_halo = gathered.at[x_hi, core, x_lo, row_z, part_h]
    tail_copy = remote(
        sig_ref.at[:, pl.ds(1792, 256)], own_halo, tail_send, tail_recv, along_y(1)
    )
    tail_copy.start()
    za_copies = []
    xb_copies = []
    for r in (2, 1, 3):
        view = gathered.at[x_hi, core, x_lo, row_z, part_a]
        za_copies.append(remote(view, view, za_send.at[r - 1], za_recv.at[r - 1], along_z(r)))
        za_copies[-1].start()
        view = gathered.at[x_hi, core, x_lo, row_z, part_b]
        xb_copies.append(remote(view, view, xb_send.at[r - 1], xb_recv.at[r - 1], along_x(r)))
        xb_copies[-1].start()

    for half in range(2):
        swapped = swap_blocks([ker_ref[u, :, half * 128:(half + 1) * 128] for u in range(16)])
        for d in range(16):
            ker_tiles[half * 16 + d] = swapped[d].astype(BF16)
    row_k = pl.multiple_of((s // 2) * 128 + x_lo * 64 + z * 16, 16)
    lane_k = pl.multiple_of((s % 2) * 128, 128)

    def send_taps(r, carry):
        d = (rank + r) % 32
        remote(
            ker_tiles.at[d], taps.at[0, y, pl.ds(row_k, 16), pl.ds(lane_k, 128)],
            ker_send, ker_recv, in_plane(d),
        ).start()
        return carry

    lax.fori_loop(1, 32, send_taps, 0)
    taps[0, y, pl.ds(row_k, 16), pl.ds(lane_k, 128)] = ker_tiles[rank]

    tail_copy.wait()
    zh_copies = []
    for r in (2, 1, 3):
        view = gathered.at[x_hi, core, x_lo, row_z, part_h]
        zh_copies.append(remote(view, view, zh_send.at[r - 1], zh_recv.at[r - 1], along_z(r)))
        zh_copies[-1].start()

    other = (y * 4 + x_hi * 2 + 1 - core, inch)
    zb_copies = {}

    def pass_b(r):
        there = (x + 4 - r) % 4
        for k in (2, 1, 3):
            view = gathered.at[there // 2, core, there % 2, row_z, part_b]
            copy = remote(view, view, zb_send.at[r, k - 1], zb_recv.at[r, k - 1], along_z(k))
            copy.start()
            zb_copies[r, k] = copy

    place = {2: 0, 1: 1, 3: 2}
    pass_b(0)
    for copy in za_copies:
        copy.wait_recv()
    xa_copies = []
    for r in (2, 1, 3):
        view = gathered.at[x_hi, core, x_lo, :, part_a]
        xa_copies.append(remote(view, view, xa_send.at[r - 1], xa_recv.at[r - 1], along_x(r)))
        xa_copies[-1].start()
    for r in (1, 3, 2):
        xb_copies[place[r]].wait_recv()
        pass_b(r)
    for copy in zh_copies:
        copy.wait_recv()
    xh_copies = []
    for r in (2, 1, 3):
        view = gathered.at[x_hi, core, x_lo, :, part_h]
        xh_copies.append(remote(view, view, xh_send.at[r - 1], xh_recv.at[r - 1], along_x(r)))
        xh_copies[-1].start()

    all_tiles = ker_tiles.at[pl.ds(0, 31)]
    pltpu.make_async_copy(all_tiles, all_tiles, ker_recv).wait()
    w_copies = []
    for r in (2, 1, 3):
        w_copies.append(remote(
            taps.at[0, y], taps.at[0, y], w_send.at[r - 1], w_recv.at[r - 1], along_y(r)
        ))
        w_copies[-1].start()

    fetch.wait()
    turn_by = (128 - (inch % 4) * 32) % 128

    def widen(k, carry):
        at = pl.ds(pl.multiple_of(k * 256, 256), 256)
        resp_wide[at, :] = pltpu.roll(resp_raw[at, :].astype(F32), turn_by, axis=1)
        return carry

    lax.fori_loop(0, 8, widen, 0)

    def merge(parts, bit):
        lane = lax.broadcasted_iota(jnp.int32, parts[0].shape, 1)
        high = (lane & (8 * bit)) != 0
        return [
            jnp.where(high, pltpu.roll(parts[i | bit], 8 * bit, axis=1), parts[i])
            for i in range(len(parts)) if not i & bit
        ]

    def pack_response(b, carry):
        for half in range(2):
            parts = [
                resp_wide[pl.ds(b * 32 + half * 16 + p, 8, stride=256), :] for p in range(16)
            ]
            parts = merge(merge(parts, 8), 4)
            parts = swap_stage(swap_stage(parts, 1), 2)
            for g in range(4):
                resp_out[g, b, :, half * 128:(half + 1) * 128] = parts[g]
        return carry

    lax.fori_loop(0, 8, pack_response, 0)
    rows_s = pl.ds(pl.multiple_of(s * 8, 8), 8)
    resp_copies = []
    for r in (1, 2, 3):
        resp_copies.append(remote(
            resp_out.at[(s + r) % 4], response.at[:, rows_s, :],
            resp_send.at[r - 1], resp_recv.at[r - 1], in_group(r),
        ))
        resp_copies[-1].start()
    response[:, rows_s, :] = resp_out[s]

    ca_copies = []
    cb_copies = []
    for r in (0, 1, 3, 2):
        there = (x + 4 - r) % 4
        if r:
            xa_copies[place[r]].wait_recv()
        view = gathered.at[there // 2, core, there % 2, :, part_a]
        ca_copies.append(remote(view, view, ca_send.at[r], ca_recv.at[r], other))
        ca_copies[-1].start()
        for k in (1, 2, 3):
            zb_copies[r, k].wait_recv()
        view = gathered.at[there // 2, core, there % 2, :, part_b]
        cb_copies.append(remote(view, view, cb_send.at[r], cb_recv.at[r], other))
        cb_copies[-1].start()
    for copy in xh_copies:
        copy.wait_recv()
    ch_copies = []
    for lo in range(2):
        view = gathered.at[1, core, lo, :, part_h]
        ch_copies.append(remote(view, view, ch_send.at[lo], ch_recv.at[lo], other))
        ch_copies[-1].start()

    def upright(hi, of_core):
        def one(k, carry):
            for m in range(8):
                lanes = pl.ds(pl.multiple_of(256 + (k * 8 + m) * 128, 128), 128)
                block = jnp.concatenate(
                    [gathered[hi, of_core, 0, :, lanes], gathered[hi, of_core, 1, :, lanes]], axis=0
                )
                rows[hi * 2 + of_core, k * 8 + m] = block.T.astype(F32)
            return carry

        lax.fori_loop(0, 2, one, 0)

    for hi in range(2):
        upright(hi, core)
    for copy in ca_copies + cb_copies + ch_copies:
        copy.wait_recv()
    for hi in range(2):
        upright(hi, 1 - core)
    at_start = y == 0
    for k in range(2):
        block = jnp.concatenate(
            [gathered[1, 1, lo, :, k * 128:(k + 1) * 128] for lo in range(2)], axis=0
        )
        halo[k * 128:(k + 1) * 128, :] = jnp.where(at_start, 0.0, block.astype(F32).T)
    for q in range(8):
        xe[:, q * 128:(q + 1) * 128] = halo[(7 - q) * 32:(8 - q) * 32, :].astype(BF16)
    first = lax.broadcasted_iota(jnp.int32, (32, 128), 0) == 0

    def order(p, carry):
        for b in range(8):
            at = pl.multiple_of((b % 4) * 32 + (p // 8) * 8, 8)
            block = jnp.concatenate(
                [rows[g, (p % 8) * 2 + b // 4, pl.ds(at, 8), :] for g in range(4)], axis=0
            )
            edge = jnp.broadcast_to(halo[pl.ds(b * 32 + p, 1), :], (32, 128))
            before = jnp.where(first, edge, pltpu.roll(block, 1, axis=0))
            sb[p, b * 32:(b + 1) * 32, :] = before.astype(BF16)
            sb[p, 256 + b * 32:256 + (b + 1) * 32, :] = block.astype(BF16)
        return carry

    lax.fori_loop(0, 32, order, 0)

    for copy in w_copies + resp_copies:
        copy.wait()

    wide_lane = lax.broadcasted_iota(jnp.int32, (256, 256), 1)
    wide_row = lax.broadcasted_iota(jnp.int32, (256, 256), 0)
    ext_lane = lax.broadcasted_iota(jnp.int32, (32, 256), 1)
    ext_row = lax.broadcasted_iota(jnp.int32, (32, 256), 0)

    def forward(turn):
        def tap_matrix():
            return jnp.concatenate([taps[turn, j] for j in range(4)], axis=0)

        acc[...] = jnp.zeros_like(acc)

        def group(g, carry):
            lhs = jnp.concatenate(
                [
                    jnp.concatenate(
                        [sb[g * WIDE + j, (8 - q) * 32:(8 - q) * 32 + 256, :] for q in range(8)],
                        axis=1,
                    )
                    for j in range(WIDE)
                ],
                axis=0,
            )
            product = jnp.dot(lhs, tap_matrix(), preferred_element_type=F32)
            here = acc[0:256, :]
            after = acc[256:512, :]
            for j in range(WIDE):
                shift = (g * WIDE + j) * 8
                turned = pltpu.roll(product[j * 256:(j + 1) * 256], shift, axis=1)
                keep = wide_lane >= shift
                here = here + jnp.where(keep, turned, 0.0)
                after = after + jnp.where(keep, 0.0, turned)
            acc[0:256, :] = here
            acc[256:512, :] = after
            return carry

        lax.fori_loop(0, 32 // WIDE, group, 0)
        edge = jnp.dot(xe[...], tap_matrix(), preferred_element_type=F32)
        edge = pltpu.roll(edge, 0, axis=1, stride=8, stride_axis=0)
        edge = jnp.sum(jnp.where(ext_lane < ext_row * 8, edge, 0.0), axis=0, keepdims=True)
        after = acc[256:512, :]
        moved = jnp.where(
            wide_row >= 32, pltpu.roll(after, 32, axis=0), pltpu.roll(after, 33, axis=0)
        )
        moved = jnp.where(wide_row == 0, jnp.broadcast_to(edge, (256, 256)), moved)
        return (acc[0:256, :] + moved) * SCALE

    def expand(resid):
        later = jnp.where(
            wide_row < 224, pltpu.roll(resid, 224, axis=0), pltpu.roll(resid, 223, axis=0)
        )
        later = jnp.where(wide_row == 255, 0.0, later)
        here_t = resid.T
        later_t = later.T
        both = jnp.concatenate([here_t, later_t], axis=0)
        r_even[...] = both.astype(BF16)
        r_odd[...] = jnp.concatenate([both[8:], both[:8]], axis=0).astype(BF16)

    def edge_windows(resid):
        line = jnp.broadcast_to(resid[0:1, :], (32, 256))
        line = pltpu.roll(line, 8, axis=1, stride=8, stride_axis=0)
        return jnp.where(ext_lane + (31 - ext_row) * 8 >= 256, line, 0.0)

    def gradient_of(one, two, edges):
        total = jnp.zeros((256, 256), F32)
        first_at = pl.multiple_of((8 - one) * 32, 32)
        second_at = pl.multiple_of((8 - two) * 32, 32)
        for g in range(8):
            left = []
            right = []
            for p in range(4 * g, 4 * g + 4):
                windows = r_odd if p % 2 else r_even
                at = 8 * (p - p % 2)
                left.append(windows[at:at + 256, :])
                right.append(jnp.concatenate(
                    [sb[p, pl.ds(first_at, 256), :], sb[p, pl.ds(second_at, 256), :]], axis=1
                ))
            total = total + jnp.dot(
                jnp.concatenate(left, axis=1), jnp.concatenate(right, axis=0),
                preferred_element_type=F32,
            )
        edge_rows = jnp.concatenate(
            [
                xe[:, pl.ds(pl.multiple_of(one * 128, 128), 128)],
                xe[:, pl.ds(pl.multiple_of(two * 128, 128), 128)],
            ],
            axis=1,
        )
        total = total + jnp.dot(edges, edge_rows, preferred_element_type=F32)
        return total.T * SCALE

    def send_energy(turn):
        energy_own[turn, 0] = jnp.full((8, 128), jnp.sum(grad_own[...] * grad_own[...]), F32)

        def send(r, carry):
            remote(
                energy_own.at[turn, 0], energy_a.at[turn, r - 1],
                ea_send.at[turn], ea_recv.at[turn], in_plane((rank + r) % 32),
            ).start()
            return carry

        lax.fori_loop(1, 32, send, 0)

    def send_tiles(turn):

        def send(r, carry):
            d = (rank + r) % 32
            to = d // 4
            rows_d = pl.multiple_of(((d % 4) // 2) * 128 + (to % 2) * 64 + (to // 2) * 16, 16)
            lanes = pl.ds(pl.multiple_of((d % 2) * 128, 128), 128)
            remote(
                taps.at[turn + 1, y, pl.ds(rows_d, 16), lanes], tiles.at[turn, rank],
                t_send.at[turn], t_recv.at[turn], in_plane(d),
            ).start()
            return carry

        lax.fori_loop(1, 32, send, 0)
        tiles[turn, rank] = taps[turn + 1, y, pl.ds(row_k, 16), pl.ds(lane_k, 128)]

    def energy_copy(turn, r):
        return remote(
            energy_own.at[turn, 1], energy_b.at[turn, r - 1],
            eb_send.at[turn, r - 1], eb_recv.at[turn, r - 1], along_y(r),
        )

    def pass_energy(turn):
        mine = energy_a.at[turn]
        pltpu.make_async_copy(mine, mine, ea_recv.at[turn]).wait()
        energy_own[turn, 1] = energy_own[turn, 0] + jnp.sum(energy_a[turn], axis=0)
        for r in (1, 2, 3):
            energy_copy(turn, r).start()

    def finish_energy(turn):
        for r in (1, 2, 3):
            energy_copy(turn, r).wait()
        total = energy_own[turn, 1] + jnp.sum(energy_b[turn], axis=0)
        factor_rows[turn + 1] = STEP_SIZE * lax.rsqrt(total / COUNT + EPSILON)

    def resid_copy(r):
        there = pl.ds(pl.multiple_of(((s + r) % 4) * 8, 8), 8)
        return remote(
            resid_all.at[:, there, :], resid_in.at[s],
            o_send.at[r - 1], o_recv.at[r - 1], in_group(r),
        )

    def shard_copy(turn, half, r):
        at = pl.ds(pl.multiple_of(half * 128, 128), 128)
        return remote(
            grad_out.at[r - 1, at], grad_in.at[r - 1, at],
            rs_send.at[turn, half, r - 1], rs_recv.at[turn, half, r - 1], along_y(r),
        )

    def gather_copy(half, r):
        view = taps.at[1, y, pl.ds(half * 128, 128)]
        return remote(view, view, ag_send.at[half, r - 1], ag_recv.at[half, r - 1], along_y(r))

    base[...] = jnp.zeros_like(base)
    factor_rows[0] = jnp.ones((8, 128), F32)

    def iterate(turn, carry):
        change = forward(turn)

        @pl.when(turn == 1)
        def _():
            finish_energy(0)

        factor = factor_rows[turn, 0:1, :]
        predicted = base[...] + jnp.concatenate([factor, factor], axis=1) * change
        base[...] = predicted
        resid = (response[...].reshape(256, 256) - predicted).astype(BF16).astype(F32)

        @pl.when(turn == 1)
        def _():
            resid_all[...] = resid.reshape(8, 32, 256)
            for r in (1, 2, 3):
                resid_copy(r).start()
            resid_in[s] = resid_all[:, rows_s, :]

        expand(resid)
        flipped = edge_windows(resid)
        edge_t[...] = jnp.concatenate(
            [flipped[31 - j:32 - j, :] for j in range(32)], axis=0
        ).T.astype(BF16)

        def chunk(j, carry):
            half = j // 2
            late = j % 2
            ahead = 2 + late
            beside = 1 - late
            part = gradient_of(
                (y + ahead) % 4 * 2 + half, (y + beside) % 4 * 2 + half, edge_t[...]
            )
            at = pl.ds(pl.multiple_of(half * 128, 128), 128)
            grad_out[ahead - 1, at] = part[0:128].astype(BF16)
            shard_copy(turn, half, ahead).start()

            @pl.when(late == 0)
            def _():
                grad_out[0, at] = part[128:256].astype(BF16)
                shard_copy(turn, half, 1).start()

            @pl.when(late == 1)
            def _():
                grad_own[at, :] = part[128:256]

            return carry

        lax.fori_loop(0, 4, chunk, 0)
        for half in range(2):
            at = slice(half * 128, (half + 1) * 128)
            for r in (1, 2, 3):
                shard_copy(turn, half, r).wait()
            own = grad_own[at, :]
            for r in range(3):
                own = own + grad_in[r, at].astype(F32)
            grad_own[at, :] = own
            taps[turn + 1, y, at] = own.astype(BF16)

            @pl.when(turn == 0)
            def _(half=half):
                for r in (2, 1, 3):
                    gather_copy(half, r).start()

        send_energy(turn)
        send_tiles(turn)
        pass_energy(turn)

        @pl.when(turn == 0)
        def _():
            for half in range(2):
                for r in (1, 3, 2):
                    gather_copy(half, r).wait()

        return carry

    lax.fori_loop(0, 2, iterate, 0)

    for r in (1, 2, 3):
        resid_copy(r).wait()

    def unpack_residual(b, carry):
        for half in range(2):
            parts = [resid_in[g, b, :, half * 128:(half + 1) * 128] for g in range(4)]
            parts = swap_stage(swap_stage(parts, 1), 2)
            for m in range(4):
                for l in range(4):
                    part = parts[l] if m == 0 else pltpu.roll(parts[l], 128 - 32 * m, axis=1)
                    at = b * 32 + half * 16 + 4 * m + l
                    resid_wide[pl.ds(at, 8, stride=256), :] = part
        return carry

    lax.fori_loop(0, 8, unpack_residual, 0)
    for k in range(16):
        flat = resid_wide[k * 128:(k + 1) * 128, :].T
        resid_ref[:, k * 128:(k + 1) * 128] = flat[0:32, :].astype(BF16)

    finish_energy(1)
    factors = [factor_rows[1, 0:1, :], factor_rows[2, 0:1, :]]
    for turn in range(2):
        half = tiles.at[turn, pl.ds(0, 31)]
        pltpu.make_async_copy(half, half, t_recv.at[turn]).wait()
    for half in range(2):
        steps = [
            factors[0] * tiles[0, half * 16 + d].astype(F32)
            + factors[1] * tiles[1, half * 16 + d].astype(F32)
            for d in range(16)
        ]
        lanes = slice(half * 128, (half + 1) * 128)
        for u, step in enumerate(swap_blocks(steps)):
            kernel_ref[u, :, lanes] = ker_ref[u, :, lanes] + step

    pltpu.make_async_copy(all_tiles, all_tiles, ker_send).wait()
    for copy in za_copies + zh_copies + xb_copies + xa_copies + xh_copies + ca_copies + cb_copies + ch_copies:
        copy.wait_send()
    for copy in zb_copies.values():
        copy.wait_send()
    for turn in range(2):
        mine = energy_a.at[turn]
        pltpu.make_async_copy(mine, mine, ea_send.at[turn]).wait()
        half = tiles.at[turn, pl.ds(0, 31)]
        pltpu.make_async_copy(half, half, t_send.at[turn]).wait()


def local(signal, response, kernel):
    dma = pltpu.SemaphoreType.DMA
    vmem = pl.BlockSpec(memory_space=pltpu.VMEM)
    kernel_out, resid = pl.pallas_call(
        body,
        out_shape=(
            jax.ShapeDtypeStruct((16, 16, 256), F32),
            jax.ShapeDtypeStruct((32, 2048), BF16),
        ),
        in_specs=[vmem, pl.BlockSpec(memory_space=pl.ANY), vmem],
        out_specs=(vmem, vmem),
        scratch_shapes=[
            pltpu.VMEM((2, 2, 2, 64, 2304), BF16),
            pltpu.VMEM((4, 16, 128, 128), F32),
            pltpu.VMEM((256, 128), F32),
            pltpu.VMEM((32, 16, 128), BF16),
            pltpu.VMEM((2048, 128), BF16),
            pltpu.VMEM((2048, 128), F32),
            pltpu.VMEM((4, 8, 8, 256), F32),
            pltpu.VMEM((2048, 128), F32),
            pltpu.VMEM((256, 256), F32),
            pltpu.VMEM((32, 512, 128), BF16),
            pltpu.VMEM((32, 1024), BF16),
            pltpu.VMEM((3, 4, 256, 256), BF16),
            pltpu.VMEM((8, 32, 256), F32),
            pltpu.VMEM((512, 256), BF16),
            pltpu.VMEM((512, 256), BF16),
            pltpu.VMEM((3, 256, 256), BF16),
            pltpu.VMEM((3, 256, 256), BF16),
            pltpu.VMEM((256, 256), F32),
            pltpu.VMEM((2, 32, 16, 128), BF16),
            pltpu.VMEM((3, 8, 128), F32),
            pltpu.VMEM((2, 31, 8, 128), F32),
            pltpu.VMEM((2, 3, 8, 128), F32),
            pltpu.VMEM((2, 2, 8, 128), F32),
            pltpu.VMEM((512, 256), F32),
            pltpu.VMEM((8, 32, 256), F32),
            pltpu.VMEM((4, 8, 8, 256), F32),
            pltpu.VMEM((256, 32), BF16),
            dma, dma, dma, dma((3,)), dma((3,)), dma, dma,
            dma((3,)), dma((3,)), dma((3,)), dma((3,)), dma((3,)), dma((3,)), dma((3,)), dma((3,)),
            dma((3,)), dma((3,)), dma((2,)), dma((2,)), dma((4, 3)), dma((4, 3)), dma((4,)), dma((4,)), dma((4,)), dma((4,)),
            dma((3,)), dma((3,)), dma((2, 2, 3)), dma((2, 2, 3)), dma((2, 3)), dma((2, 3)),
            dma((2,)), dma((2,)), dma((2, 3)), dma((2, 3)), dma((2,)), dma((2,)), dma((3,)), dma((3,)),
        ],
        compiler_params=pltpu.CompilerParams(
            collective_id=0, has_side_effects=True, vmem_limit_bytes=60 * 2**20
        ),
    )(signal.T, response, kernel)
    return kernel_out, resid.T


def solution(mesh):
    placed = (P("tm", "inch"), P("tm", None), P("tm", "inch", None))
    return jax.shard_map(
        local,
        mesh=mesh,
        in_specs=placed,
        out_specs=(P("tm", "inch", None), P("tm", "inch")),
        check_vma=False,
    )
```

```python
import math

import jax
import jax.numpy as jnp
from jax import lax
from jax.experimental import pallas as pl
from jax.experimental.pallas import tpu as pltpu
from jax.sharding import PartitionSpec as P

STEP_SIZE = 0.5
EPSILON = 1e-06
F32 = jnp.float32
BF16 = jnp.bfloat16
MESH = pl.DeviceIdType.MESH
TAPS = 256
CI = 128
CO = 256
SCALE = 1.0 / math.sqrt(TAPS * CI)
COUNT = TAPS * CI * CO


def remote(src, dst, send, recv, device):
    return pltpu.make_async_remote_copy(
        src_ref=src, dst_ref=dst, send_sem=send, recv_sem=recv,
        device_id=device, device_id_type=MESH,
    )


def swap_blocks(parts):
    parts = list(parts)
    for bit in (1, 2, 4, 8):
        parts = swap_stage(parts, bit)
    return parts


def swap_stage(parts, bit):
    lane = lax.broadcasted_iota(jnp.int32, parts[0].shape, 1)
    high = (lane & (8 * bit)) != 0
    result = list(parts)
    for i in range(len(parts)):
        if not i & bit:
            low_part, high_part = parts[i], parts[i | bit]
            result[i] = jnp.where(high, pltpu.roll(high_part, 8 * bit, axis=1), low_part)
            result[i | bit] = jnp.where(
                high, high_part, pltpu.roll(low_part, 128 - 8 * bit, axis=1)
            )
    return result


def body(
    sig_hbm, resp_hbm, ker_hbm,
    kernel_ref, resid_ref,
    gathered, rows, halo, ker_tiles, resp_raw, resp_wide, resp_out, resid_wide, base,
    sb, xe, taps, response, r_even, r_odd,
    grad_out, grad_in, grad_own, tiles, factor_rows, energy_a, energy_b, energy_own, resid_all,
    resid_in, edge_t,
    sig_ref, ker_ref, in_sem,
    hbm_sem, ker_send, ker_recv, resp_send, resp_recv, tail_send, tail_recv,
    za_send, za_recv, zh_send, zh_recv, xb_send, xb_recv, xa_send, xa_recv,
    xh_send, xh_recv, ch_send, ch_recv, zb_send, zb_recv, ca_send, ca_recv, cb_send, cb_recv,
    w_send, w_recv, rs_send, rs_recv, ag_send, ag_recv,
    ea_send, ea_recv, eb_send, eb_recv, t_send, t_recv, o_send, o_recv,
):
    tm = lax.axis_index("tm")
    inch = lax.axis_index("inch")
    y = tm // 4
    s = tm % 4
    x_hi = s // 2
    core = s % 2
    z = inch // 2
    x_lo = inch % 2
    x = x_hi * 2 + x_lo
    rank = inch * 4 + s

    def in_plane(d):
        return (y * 4 + d % 4, d // 4)

    def along_y(r):
        return ((((y + r) % 4) * 4) + s, inch)

    def along_z(r):
        return (tm, ((z + r) % 4) * 2 + x_lo)

    def along_x(r):
        there = (x + r) % 4
        return (y * 4 + (there // 2) * 2 + core, z * 2 + there % 2)

    def in_group(r):
        return (y * 4 + (s + r) % 4, inch)

    barrier = pltpu.get_barrier_semaphore()

    def greet(r, carry):
        pl.semaphore_signal(
            barrier, inc=1, device_id=in_plane((rank + r) % 32), device_id_type=MESH
        )
        return carry

    lax.fori_loop(1, 32, greet, 0)
    for r in (1, 2, 3):
        pl.semaphore_signal(barrier, inc=1, device_id=along_y(r), device_id_type=MESH)

    take_sig = pltpu.make_async_copy(sig_hbm, sig_ref, in_sem.at[0])
    take_sig.start()
    take_ker = pltpu.make_async_copy(ker_hbm, ker_ref, in_sem.at[1])
    take_ker.start()
    columns = pl.ds(pl.multiple_of((inch // 4) * 128, 128), 128)
    fetch = pltpu.make_async_copy(resp_hbm.at[:, columns], resp_raw, hbm_sem)
    fetch.start()
    row_z = pl.ds(pl.multiple_of(z * 16, 16), 16)
    take_sig.wait()
    lane16 = lax.broadcasted_iota(jnp.int32, (16, 128), 1)
    parts = [sig_ref[:, k * 128:(k + 1) * 128].astype(F32) for k in range(16)]
    for bit in (1, 2, 4):
        high = (lane16 & bit) != 0
        for i in range(16):
            if not i & (2 * bit):
                one, two = parts[i], parts[i | (2 * bit)]
                parts[i] = jnp.where(high, pltpu.roll(two, bit, axis=1), one)
                parts[i | (2 * bit)] = jnp.where(high, two, pltpu.roll(one, 128 - bit, axis=1))
    for k in range(16):
        gathered[x_hi, core, x_lo, row_z, 256 + k * 128:384 + k * 128] = parts[k].astype(BF16)
    part_h, part_a, part_b = pl.ds(0, 256), pl.ds(256, 1024), pl.ds(1280, 1024)

    pl.semaphore_wait(barrier, 34)

    own_halo = gathered.at[x_hi, core, x_lo, row_z, part_h]
    tail_copy = remote(
        sig_ref.at[:, pl.ds(1792, 256)], own_halo, tail_send, tail_recv, along_y(1)
    )
    tail_copy.start()
    za_copies = []
    xb_copies = []
    for r in (2, 1, 3):
        view = gathered.at[x_hi, core, x_lo, row_z, part_a]
        za_copies.append(remote(view, view, za_send.at[r - 1], za_recv.at[r - 1], along_z(r)))
        za_copies[-1].start()
        view = gathered.at[x_hi, core, x_lo, row_z, part_b]
        xb_copies.append(remote(view, view, xb_send.at[r - 1], xb_recv.at[r - 1], along_x(r)))
        xb_copies[-1].start()

    take_ker.wait()
    for half in range(2):
        swapped = swap_blocks([ker_ref[u, :, half * 128:(half + 1) * 128] for u in range(16)])
        for d in range(16):
            ker_tiles[half * 16 + d] = swapped[d].astype(BF16)
    row_k = pl.multiple_of((s // 2) * 128 + x_lo * 64 + z * 16, 16)
    lane_k = pl.multiple_of((s % 2) * 128, 128)

    def send_taps(r, carry):
        d = (rank + r) % 32
        remote(
            ker_tiles.at[d], taps.at[0, y, pl.ds(row_k, 16), pl.ds(lane_k, 128)],
            ker_send, ker_recv, in_plane(d),
        ).start()
        return carry

    lax.fori_loop(1, 32, send_taps, 0)
    taps[0, y, pl.ds(row_k, 16), pl.ds(lane_k, 128)] = ker_tiles[rank]

    tail_copy.wait()
    zh_copies = []
    for r in (2, 1, 3):
        view = gathered.at[x_hi, core, x_lo, row_z, part_h]
        zh_copies.append(remote(view, view, zh_send.at[r - 1], zh_recv.at[r - 1], along_z(r)))
        zh_copies[-1].start()

    other = (y * 4 + x_hi * 2 + 1 - core, inch)
    zb_copies = {}

    def pass_b(r):
        there = (x + 4 - r) % 4
        for k in (2, 1, 3):
            view = gathered.at[there // 2, core, there % 2, row_z, part_b]
            copy = remote(view, view, zb_send.at[r, k - 1], zb_recv.at[r, k - 1], along_z(k))
            copy.start()
            zb_copies[r, k] = copy

    place = {2: 0, 1: 1, 3: 2}
    pass_b(0)
    for copy in za_copies:
        copy.wait_recv()
    xa_copies = []
    for r in (2, 1, 3):
        view = gathered.at[x_hi, core, x_lo, :, part_a]
        xa_copies.append(remote(view, view, xa_send.at[r - 1], xa_recv.at[r - 1], along_x(r)))
        xa_copies[-1].start()
    for r in (1, 3, 2):
        xb_copies[place[r]].wait_recv()
        pass_b(r)
    for copy in zh_copies:
        copy.wait_recv()
    xh_copies = []
    for r in (2, 1, 3):
        view = gathered.at[x_hi, core, x_lo, :, part_h]
        xh_copies.append(remote(view, view, xh_send.at[r - 1], xh_recv.at[r - 1], along_x(r)))
        xh_copies[-1].start()

    all_tiles = ker_tiles.at[pl.ds(0, 31)]
    pltpu.make_async_copy(all_tiles, all_tiles, ker_recv).wait()
    w_copies = []
    for r in (2, 1, 3):
        w_copies.append(remote(
            taps.at[0, y], taps.at[0, y], w_send.at[r - 1], w_recv.at[r - 1], along_y(r)
        ))
        w_copies[-1].start()

    fetch.wait()
    turn_by = (128 - (inch % 4) * 32) % 128

    def widen(k, carry):
        at = pl.ds(pl.multiple_of(k * 256, 256), 256)
        resp_wide[at, :] = pltpu.roll(resp_raw[at, :].astype(F32), turn_by, axis=1)
        return carry

    lax.fori_loop(0, 8, widen, 0)

    def merge(parts, bit):
        lane = lax.broadcasted_iota(jnp.int32, parts[0].shape, 1)
        high = (lane & (8 * bit)) != 0
        return [
            jnp.where(high, pltpu.roll(parts[i | bit], 8 * bit, axis=1), parts[i])
            for i in range(len(parts)) if not i & bit
        ]

    def pack_response(b, carry):
        for half in range(2):
            parts = [
                resp_wide[pl.ds(b * 32 + half * 16 + p, 8, stride=256), :] for p in range(16)
            ]
            parts = merge(merge(parts, 8), 4)
            parts = swap_stage(swap_stage(parts, 1), 2)
            for g in range(4):
                resp_out[g, b, :, half * 128:(half + 1) * 128] = parts[g]
        return carry

    lax.fori_loop(0, 8, pack_response, 0)
    rows_s = pl.ds(pl.multiple_of(s * 8, 8), 8)
    resp_copies = []
    for r in (1, 2, 3):
        resp_copies.append(remote(
            resp_out.at[(s + r) % 4], response.at[:, rows_s, :],
            resp_send.at[r - 1], resp_recv.at[r - 1], in_group(r),
        ))
        resp_copies[-1].start()
    response[:, rows_s, :] = resp_out[s]

    ca_copies = []
    cb_copies = []
    for r in (0, 1, 3, 2):
        there = (x + 4 - r) % 4
        if r:
            xa_copies[place[r]].wait_recv()
        view = gathered.at[there // 2, core, there % 2, :, part_a]
        ca_copies.append(remote(view, view, ca_send.at[r], ca_recv.at[r], other))
        ca_copies[-1].start()
        for k in (1, 2, 3):
            zb_copies[r, k].wait_recv()
        view = gathered.at[there // 2, core, there % 2, :, part_b]
        cb_copies.append(remote(view, view, cb_send.at[r], cb_recv.at[r], other))
        cb_copies[-1].start()
    for copy in xh_copies:
        copy.wait_recv()
    ch_copies = []
    for lo in range(2):
        view = gathered.at[1, core, lo, :, part_h]
        ch_copies.append(remote(view, view, ch_send.at[lo], ch_recv.at[lo], other))
        ch_copies[-1].start()

    def upright(hi, of_core):
        def one(k, carry):
            for m in range(8):
                lanes = pl.ds(pl.multiple_of(256 + (k * 8 + m) * 128, 128), 128)
                block = jnp.concatenate(
                    [gathered[hi, of_core, 0, :, lanes], gathered[hi, of_core, 1, :, lanes]], axis=0
                )
                rows[hi * 2 + of_core, k * 8 + m] = block.T.astype(F32)
            return carry

        lax.fori_loop(0, 2, one, 0)

    for hi in range(2):
        upright(hi, core)
    for copy in ca_copies + cb_copies + ch_copies:
        copy.wait_recv()
    for hi in range(2):
        upright(hi, 1 - core)
    at_start = y == 0
    for k in range(2):
        block = jnp.concatenate(
            [gathered[1, 1, lo, :, k * 128:(k + 1) * 128] for lo in range(2)], axis=0
        )
        halo[k * 128:(k + 1) * 128, :] = jnp.where(at_start, 0.0, block.astype(F32).T)
    for q in range(8):
        xe[:, q * 128:(q + 1) * 128] = halo[(7 - q) * 32:(8 - q) * 32, :].astype(BF16)
    first = lax.broadcasted_iota(jnp.int32, (32, 128), 0) == 0

    def order(p, carry):
        for b in range(8):
            at = pl.multiple_of((b % 4) * 32 + (p // 8) * 8, 8)
            block = jnp.concatenate(
                [rows[g, (p % 8) * 2 + b // 4, pl.ds(at, 8), :] for g in range(4)], axis=0
            )
            edge = jnp.broadcast_to(halo[pl.ds(b * 32 + p, 1), :], (32, 128))
            before = jnp.where(first, edge, pltpu.roll(block, 1, axis=0))
            sb[p, b * 32:(b + 1) * 32, :] = before.astype(BF16)
            sb[p, 256 + b * 32:256 + (b + 1) * 32, :] = block.astype(BF16)
        return carry

    lax.fori_loop(0, 32, order, 0)

    for copy in w_copies + resp_copies:
        copy.wait()

    wide_lane = lax.broadcasted_iota(jnp.int32, (256, 256), 1)
    wide_row = lax.broadcasted_iota(jnp.int32, (256, 256), 0)
    ext_lane = lax.broadcasted_iota(jnp.int32, (32, 256), 1)
    ext_row = lax.broadcasted_iota(jnp.int32, (32, 256), 0)

    def forward(turn):
        def tap_matrix():
            return jnp.concatenate([taps[turn, j] for j in range(4)], axis=0)

        lhs = jnp.concatenate(
            [
                jnp.concatenate(
                    [sb[p, (8 - q) * 32:(8 - q) * 32 + 256, :] for q in range(8)], axis=1
                )
                for p in range(32)
            ],
            axis=0,
        )
        product = jnp.dot(lhs, tap_matrix(), preferred_element_type=F32)
        here = product[0:256]
        after = jnp.zeros((256, 256), F32)
        for p in range(1, 32):
            turned = pltpu.roll(product[p * 256:(p + 1) * 256], 8 * p, axis=1)
            keep = wide_lane >= 8 * p
            here = here + jnp.where(keep, turned, 0.0)
            after = after + jnp.where(keep, 0.0, turned)
        edge = jnp.dot(xe[...], tap_matrix(), preferred_element_type=F32)
        edge = pltpu.roll(edge, 0, axis=1, stride=8, stride_axis=0)
        edge = jnp.sum(jnp.where(ext_lane < ext_row * 8, edge, 0.0), axis=0, keepdims=True)
        moved = jnp.where(
            wide_row >= 32, pltpu.roll(after, 32, axis=0), pltpu.roll(after, 33, axis=0)
        )
        moved = jnp.where(wide_row == 0, jnp.broadcast_to(edge, (256, 256)), moved)
        return (here + moved) * SCALE

    def expand(resid):
        later = jnp.where(
            wide_row < 224, pltpu.roll(resid, 224, axis=0), pltpu.roll(resid, 223, axis=0)
        )
        later = jnp.where(wide_row == 255, 0.0, later)
        here_t = resid.T
        later_t = later.T
        both = jnp.concatenate([here_t, later_t], axis=0)
        r_even[...] = both.astype(BF16)
        r_odd[...] = jnp.concatenate([both[8:], both[:8]], axis=0).astype(BF16)

    def edge_windows(resid):
        line = jnp.broadcast_to(resid[0:1, :], (32, 256))
        line = pltpu.roll(line, 8, axis=1, stride=8, stride_axis=0)
        return jnp.where(ext_lane + (31 - ext_row) * 8 >= 256, line, 0.0)

    def gradient_of(one, two, edges):
        total = jnp.zeros((256, 256), F32)
        first_at = pl.multiple_of((8 - one) * 32, 32)
        second_at = pl.multiple_of((8 - two) * 32, 32)
        for g in range(8):
            left = []
            right = []
            for p in range(4 * g, 4 * g + 4):
                windows = r_odd if p % 2 else r_even
                at = 8 * (p - p % 2)
                left.append(windows[at:at + 256, :])
                right.append(jnp.concatenate(
                    [sb[p, pl.ds(first_at, 256), :], sb[p, pl.ds(second_at, 256), :]], axis=1
                ))
            total = total + jnp.dot(
                jnp.concatenate(left, axis=1), jnp.concatenate(right, axis=0),
                preferred_element_type=F32,
            )
        edge_rows = jnp.concatenate(
            [
                xe[:, pl.ds(pl.multiple_of(one * 128, 128), 128)],
                xe[:, pl.ds(pl.multiple_of(two * 128, 128), 128)],
            ],
            axis=1,
        )
        total = total + jnp.dot(edges, edge_rows, preferred_element_type=F32)
        return total.T * SCALE

    def send_energy(turn):
        energy_own[turn, 0] = jnp.full((8, 128), jnp.sum(grad_own[...] * grad_own[...]), F32)

        def send(r, carry):
            remote(
                energy_own.at[turn, 0], energy_a.at[turn, r - 1],
                ea_send.at[turn], ea_recv.at[turn], in_plane((rank + r) % 32),
            ).start()
            return carry

        lax.fori_loop(1, 32, send, 0)

    def send_tiles(turn):

        def send(r, carry):
            d = (rank + r) % 32
            to = d // 4
            rows_d = pl.multiple_of(((d % 4) // 2) * 128 + (to % 2) * 64 + (to // 2) * 16, 16)
            lanes = pl.ds(pl.multiple_of((d % 2) * 128, 128), 128)
            remote(
                taps.at[turn + 1, y, pl.ds(rows_d, 16), lanes], tiles.at[turn, rank],
                t_send.at[turn], t_recv.at[turn], in_plane(d),
            ).start()
            return carry

        lax.fori_loop(1, 32, send, 0)
        tiles[turn, rank] = taps[turn + 1, y, pl.ds(row_k, 16), pl.ds(lane_k, 128)]

    def energy_copy(turn, r):
        return remote(
            energy_own.at[turn, 1], energy_b.at[turn, r - 1],
            eb_send.at[turn, r - 1], eb_recv.at[turn, r - 1], along_y(r),
        )

    def pass_energy(turn):
        mine = energy_a.at[turn]
        pltpu.make_async_copy(mine, mine, ea_recv.at[turn]).wait()
        energy_own[turn, 1] = energy_own[turn, 0] + jnp.sum(energy_a[turn], axis=0)
        for r in (1, 2, 3):
            energy_copy(turn, r).start()

    def finish_energy(turn):
        for r in (1, 2, 3):
            energy_copy(turn, r).wait()
        total = energy_own[turn, 1] + jnp.sum(energy_b[turn], axis=0)
        factor_rows[turn + 1] = STEP_SIZE * lax.rsqrt(total / COUNT + EPSILON)

    def resid_copy(r):
        there = pl.ds(pl.multiple_of(((s + r) % 4) * 8, 8), 8)
        return remote(
            resid_all.at[:, there, :], resid_in.at[s],
            o_send.at[r - 1], o_recv.at[r - 1], in_group(r),
        )

    def shard_copy(turn, half, r):
        at = pl.ds(pl.multiple_of(half * 128, 128), 128)
        return remote(
            grad_out.at[r - 1, at], grad_in.at[r - 1, at],
            rs_send.at[turn, half, r - 1], rs_recv.at[turn, half, r - 1], along_y(r),
        )

    def gather_copy(half, r):
        view = taps.at[1, y, pl.ds(half * 128, 128)]
        return remote(view, view, ag_send.at[half, r - 1], ag_recv.at[half, r - 1], along_y(r))

    base[...] = jnp.zeros_like(base)
    factor_rows[0] = jnp.ones((8, 128), F32)

    def iterate(turn, carry):
        change = forward(turn)

        @pl.when(turn == 1)
        def _():
            finish_energy(0)

        factor = factor_rows[turn, 0:1, :]
        predicted = base[...] + jnp.concatenate([factor, factor], axis=1) * change
        base[...] = predicted
        resid = (response[...].reshape(256, 256) - predicted).astype(BF16).astype(F32)

        @pl.when(turn == 1)
        def _():
            resid_all[...] = resid.reshape(8, 32, 256)
            for r in (1, 2, 3):
                resid_copy(r).start()
            resid_in[s] = resid_all[:, rows_s, :]

        expand(resid)
        flipped = edge_windows(resid)
        edge_t[...] = jnp.concatenate(
            [flipped[31 - j:32 - j, :] for j in range(32)], axis=0
        ).T.astype(BF16)

        def chunk(j, carry):
            half = j // 2
            late = j % 2
            ahead = 2 + late
            beside = 1 - late
            part = gradient_of(
                (y + ahead) % 4 * 2 + half, (y + beside) % 4 * 2 + half, edge_t[...]
            )
            at = pl.ds(pl.multiple_of(half * 128, 128), 128)
            grad_out[ahead - 1, at] = part[0:128].astype(BF16)
            shard_copy(turn, half, ahead).start()

            @pl.when(late == 0)
            def _():
                grad_out[0, at] = part[128:256].astype(BF16)
                shard_copy(turn, half, 1).start()

            @pl.when(late == 1)
            def _():
                grad_own[at, :] = part[128:256]

            return carry

        lax.fori_loop(0, 4, chunk, 0)

        @pl.when(turn == 1)
        def _():
            send_tiles(0)

        for half in range(2):
            at = slice(half * 128, (half + 1) * 128)
            for r in (1, 2, 3):
                shard_copy(turn, half, r).wait()
            own = grad_own[at, :]
            for r in range(3):
                own = own + grad_in[r, at].astype(F32)
            grad_own[at, :] = own
            taps[turn + 1, y, at] = own.astype(BF16)

            @pl.when(turn == 0)
            def _(half=half):
                for r in (2, 1, 3):
                    gather_copy(half, r).start()

        send_energy(turn)

        @pl.when(turn == 1)
        def _():
            send_tiles(1)

        pass_energy(turn)

        @pl.when(turn == 0)
        def _():
            for half in range(2):
                for r in (1, 3, 2):
                    gather_copy(half, r).wait()

        return carry

    lax.fori_loop(0, 2, iterate, 0)

    for r in (1, 2, 3):
        resid_copy(r).wait()

    def unpack_residual(b, carry):
        for half in range(2):
            parts = [resid_in[g, b, :, half * 128:(half + 1) * 128] for g in range(4)]
            parts = swap_stage(swap_stage(parts, 1), 2)
            for m in range(4):
                for l in range(4):
                    part = parts[l] if m == 0 else pltpu.roll(parts[l], 128 - 32 * m, axis=1)
                    at = b * 32 + half * 16 + 4 * m + l
                    resid_wide[pl.ds(at, 8, stride=256), :] = part
        return carry

    lax.fori_loop(0, 8, unpack_residual, 0)
    for k in range(16):
        flat = resid_wide[k * 128:(k + 1) * 128, :].T
        resid_ref[:, k * 128:(k + 1) * 128] = flat[0:32, :].astype(BF16)

    finish_energy(1)
    factors = [factor_rows[1, 0:1, :], factor_rows[2, 0:1, :]]
    for turn in range(2):
        half = tiles.at[turn, pl.ds(0, 31)]
        pltpu.make_async_copy(half, half, t_recv.at[turn]).wait()
    for half in range(2):
        steps = [
            factors[0] * tiles[0, half * 16 + d].astype(F32)
            + factors[1] * tiles[1, half * 16 + d].astype(F32)
            for d in range(16)
        ]
        lanes = slice(half * 128, (half + 1) * 128)
        for u, step in enumerate(swap_blocks(steps)):
            kernel_ref[u, :, lanes] = step

    pltpu.make_async_copy(all_tiles, all_tiles, ker_send).wait()
    for copy in za_copies + zh_copies + xb_copies + xa_copies + xh_copies + ca_copies + cb_copies + ch_copies:
        copy.wait_send()
    for copy in zb_copies.values():
        copy.wait_send()
    for turn in range(2):
        mine = energy_a.at[turn]
        pltpu.make_async_copy(mine, mine, ea_send.at[turn]).wait()
        half = tiles.at[turn, pl.ds(0, 31)]
        pltpu.make_async_copy(half, half, t_send.at[turn]).wait()


def finish(step_ref, ker_ref, resid_in_ref, kernel_ref, resid_ref):
    kernel_ref[...] = ker_ref[...] + step_ref[...]
    resid_ref[...] = resid_in_ref[...]


def local(signal, response, kernel):
    dma = pltpu.SemaphoreType.DMA
    vmem = pl.BlockSpec(memory_space=pltpu.VMEM)
    kernel_out, resid = pl.pallas_call(
        body,
        out_shape=(
            jax.ShapeDtypeStruct((16, 16, 256), F32),
            jax.ShapeDtypeStruct((32, 2048), BF16),
        ),
        in_specs=[pl.BlockSpec(memory_space=pl.ANY)] * 3,
        out_specs=(vmem, vmem),
        scratch_shapes=[
            pltpu.VMEM((2, 2, 2, 64, 2304), BF16),
            pltpu.VMEM((4, 16, 128, 128), F32),
            pltpu.VMEM((256, 128), F32),
            pltpu.VMEM((32, 16, 128), BF16),
            pltpu.VMEM((2048, 128), BF16),
            pltpu.VMEM((2048, 128), F32),
            pltpu.VMEM((4, 8, 8, 256), F32),
            pltpu.VMEM((2048, 128), F32),
            pltpu.VMEM((256, 256), F32),
            pltpu.VMEM((32, 512, 128), BF16),
            pltpu.VMEM((32, 1024), BF16),
            pltpu.VMEM((3, 4, 256, 256), BF16),
            pltpu.VMEM((8, 32, 256), F32),
            pltpu.VMEM((512, 256), BF16),
            pltpu.VMEM((512, 256), BF16),
            pltpu.VMEM((3, 256, 256), BF16),
            pltpu.VMEM((3, 256, 256), BF16),
            pltpu.VMEM((256, 256), F32),
            pltpu.VMEM((2, 32, 16, 128), BF16),
            pltpu.VMEM((3, 8, 128), F32),
            pltpu.VMEM((2, 31, 8, 128), F32),
            pltpu.VMEM((2, 3, 8, 128), F32),
            pltpu.VMEM((2, 2, 8, 128), F32),
            pltpu.VMEM((8, 32, 256), F32),
            pltpu.VMEM((4, 8, 8, 256), F32),
            pltpu.VMEM((256, 32), BF16),
            pltpu.VMEM((16, 2048), BF16),
            pltpu.VMEM((16, 16, 256), F32),
            dma((2,)),
            dma, dma, dma, dma((3,)), dma((3,)), dma, dma,
            dma((3,)), dma((3,)), dma((3,)), dma((3,)), dma((3,)), dma((3,)), dma((3,)), dma((3,)),
            dma((3,)), dma((3,)), dma((2,)), dma((2,)), dma((4, 3)), dma((4, 3)), dma((4,)), dma((4,)), dma((4,)), dma((4,)),
            dma((3,)), dma((3,)), dma((2, 2, 3)), dma((2, 2, 3)), dma((2, 3)), dma((2, 3)),
            dma((2,)), dma((2,)), dma((2, 3)), dma((2, 3)), dma((2,)), dma((2,)), dma((3,)), dma((3,)),
        ],
        compiler_params=pltpu.CompilerParams(
            collective_id=0, has_side_effects=True, vmem_limit_bytes=60 * 2**20
        ),
    )(signal.T, response, kernel)
    kernel_out, resid = pl.pallas_call(
        finish,
        out_shape=(
            jax.ShapeDtypeStruct((16, 16, 256), F32),
            jax.ShapeDtypeStruct((32, 2048), BF16),
        ),
        in_specs=[vmem] * 3,
        out_specs=(vmem, vmem),
    )(kernel_out, kernel, resid)
    return kernel_out, resid.T


def solution(mesh):
    placed = (P("tm", "inch"), P("tm", None), P("tm", "inch", None))
    return jax.shard_map(
        local,
        mesh=mesh,
        in_specs=placed,
        out_specs=(P("tm", "inch", None), P("tm", "inch")),
        check_vma=False,
    )
```

```python
import math

import jax
import jax.numpy as jnp
from jax import lax
from jax.experimental import pallas as pl
from jax.experimental.pallas import tpu as pltpu
from jax.sharding import PartitionSpec as P

STEP_SIZE = 0.5
EPSILON = 1e-06
F32 = jnp.float32
BF16 = jnp.bfloat16
MESH = pl.DeviceIdType.MESH
TAPS = 256
CI = 128
CO = 256
SCALE = 1.0 / math.sqrt(TAPS * CI)
COUNT = TAPS * CI * CO


def remote(src, dst, send, recv, device):
    return pltpu.make_async_remote_copy(
        src_ref=src, dst_ref=dst, send_sem=send, recv_sem=recv,
        device_id=device, device_id_type=MESH,
    )


def swap_blocks(parts):
    parts = list(parts)
    for bit in (1, 2, 4, 8):
        parts = swap_stage(parts, bit)
    return parts


def swap_stage(parts, bit):
    lane = lax.broadcasted_iota(jnp.int32, parts[0].shape, 1)
    high = (lane & (8 * bit)) != 0
    result = list(parts)
    for i in range(len(parts)):
        if not i & bit:
            low_part, high_part = parts[i], parts[i | bit]
            result[i] = jnp.where(high, pltpu.roll(high_part, 8 * bit, axis=1), low_part)
            result[i | bit] = jnp.where(
                high, high_part, pltpu.roll(low_part, 128 - 8 * bit, axis=1)
            )
    return result


def body(
    sig_hbm, resp_hbm, ker_hbm,
    kernel_ref, resid_ref,
    gathered, rows, halo, ker_tiles, resp_raw, resp_wide, resp_out, resid_wide, base,
    sb, xe, taps, response, r_even, r_odd,
    grad_out, grad_in, grad_own, tiles, factor_rows, energy_a, energy_b, energy_own, resid_all,
    resid_in, edge_t,
    sig_ref, ker_ref, in_sem,
    hbm_sem, ker_send, ker_recv, resp_send, resp_recv, tail_send, tail_recv,
    za_send, za_recv, xb_send, xb_recv, xa_send, xa_recv,
    halo_send, halo_recv, zb_send, zb_recv, ca_send, ca_recv, cb_send, cb_recv,
    w_send, w_recv, rs_send, rs_recv, ag_send, ag_recv,
    ea_send, ea_recv, eb_send, eb_recv, t_send, t_recv, o_send, o_recv,
):
    tm = lax.axis_index("tm")
    inch = lax.axis_index("inch")
    y = tm // 4
    s = tm % 4
    x_hi = s // 2
    core = s % 2
    z = inch // 2
    x_lo = inch % 2
    x = x_hi * 2 + x_lo
    rank = inch * 4 + s

    def in_plane(d):
        return (y * 4 + d % 4, d // 4)

    def along_y(r):
        return ((((y + r) % 4) * 4) + s, inch)

    def along_z(r):
        return (tm, ((z + r) % 4) * 2 + x_lo)

    def diagonal(r, k):
        return (((y + r) % 4) * 4 + s, ((z + k) % 4) * 2 + x_lo)

    def in_row(g):
        return (y * 4 + (g // 4) * 2 + g % 2, z * 2 + (g // 2) % 2)

    def along_x(r):
        there = (x + r) % 4
        return (y * 4 + (there // 2) * 2 + core, z * 2 + there % 2)

    def in_group(r):
        return (y * 4 + (s + r) % 4, inch)

    barrier = pltpu.get_barrier_semaphore()

    def greet(r, carry):
        pl.semaphore_signal(
            barrier, inc=1, device_id=in_plane((rank + r) % 32), device_id_type=MESH
        )
        return carry

    lax.fori_loop(1, 32, greet, 0)
    for r in (1, 2, 3):
        pl.semaphore_signal(barrier, inc=1, device_id=along_y(r), device_id_type=MESH)
        pl.semaphore_signal(barrier, inc=1, device_id=diagonal(3, r), device_id_type=MESH)

    take_sig = pltpu.make_async_copy(sig_hbm, sig_ref, in_sem.at[0])
    take_sig.start()
    take_ker = pltpu.make_async_copy(ker_hbm, ker_ref, in_sem.at[1])
    take_ker.start()
    columns = pl.ds(pl.multiple_of((inch // 4) * 128, 128), 128)
    fetch = pltpu.make_async_copy(resp_hbm.at[:, columns], resp_raw, hbm_sem)
    fetch.start()
    row_z = pl.ds(pl.multiple_of(z * 16, 16), 16)
    take_sig.wait()
    lane16 = lax.broadcasted_iota(jnp.int32, (16, 128), 1)
    parts = [sig_ref[:, k * 128:(k + 1) * 128].astype(F32) for k in range(16)]
    for bit in (1, 2, 4):
        high = (lane16 & bit) != 0
        for i in range(16):
            if not i & (2 * bit):
                one, two = parts[i], parts[i | (2 * bit)]
                parts[i] = jnp.where(high, pltpu.roll(two, bit, axis=1), one)
                parts[i | (2 * bit)] = jnp.where(high, two, pltpu.roll(one, 128 - bit, axis=1))
    for k in range(16):
        gathered[x_hi, core, x_lo, row_z, 256 + k * 128:384 + k * 128] = parts[k].astype(BF16)
    part_h, part_a, part_b = pl.ds(0, 256), pl.ds(256, 1024), pl.ds(1280, 1024)

    pl.semaphore_wait(barrier, 37)

    own_halo = gathered.at[x_hi, core, x_lo, row_z, part_h]
    tail_copies = []
    for k in (2, 1, 3, 0):
        tail_copies.append(remote(
            sig_ref.at[:, pl.ds(1792, 256)], own_halo,
            tail_send.at[k], tail_recv.at[k], diagonal(1, k),
        ))
        tail_copies[-1].start()
    za_copies = []
    xb_copies = []
    for r in (2, 1, 3):
        view = gathered.at[x_hi, core, x_lo, row_z, part_a]
        za_copies.append(remote(view, view, za_send.at[r - 1], za_recv.at[r - 1], along_z(r)))
        za_copies[-1].start()
        view = gathered.at[x_hi, core, x_lo, row_z, part_b]
        xb_copies.append(remote(view, view, xb_send.at[r - 1], xb_recv.at[r - 1], along_x(r)))
        xb_copies[-1].start()

    take_ker.wait()
    for half in range(2):
        swapped = swap_blocks([ker_ref[u, :, half * 128:(half + 1) * 128] for u in range(16)])
        for d in range(16):
            ker_tiles[half * 16 + d] = swapped[d].astype(BF16)
    row_k = pl.multiple_of((s // 2) * 128 + x_lo * 64 + z * 16, 16)
    lane_k = pl.multiple_of((s % 2) * 128, 128)

    def send_taps(r, carry):
        d = (rank + r) % 32
        remote(
            ker_tiles.at[d], taps.at[0, y, pl.ds(row_k, 16), pl.ds(lane_k, 128)],
            ker_send, ker_recv, in_plane(d),
        ).start()
        return carry

    lax.fori_loop(1, 32, send_taps, 0)
    taps[0, y, pl.ds(row_k, 16), pl.ds(lane_k, 128)] = ker_tiles[rank]

    other = (y * 4 + x_hi * 2 + 1 - core, inch)
    zb_copies = {}

    def pass_b(r):
        there = (x + 4 - r) % 4
        for k in (2, 1, 3):
            view = gathered.at[there // 2, core, there % 2, row_z, part_b]
            copy = remote(view, view, zb_send.at[r, k - 1], zb_recv.at[r, k - 1], along_z(k))
            copy.start()
            zb_copies[r, k] = copy

    place = {2: 0, 1: 1, 3: 2}
    pass_b(0)
    for copy in za_copies:
        copy.wait_recv()
    xa_copies = []
    for r in (2, 1, 3):
        view = gathered.at[x_hi, core, x_lo, :, part_a]
        xa_copies.append(remote(view, view, xa_send.at[r - 1], xa_recv.at[r - 1], along_x(r)))
        xa_copies[-1].start()
    view = gathered.at[x_hi, core, x_lo, :, part_a]
    ca_copies = [remote(view, view, ca_send.at[0], ca_recv.at[0], other)]
    ca_copies[0].start()
    for r in (1, 3, 2):
        xb_copies[place[r]].wait_recv()
        pass_b(r)

    for copy in tail_copies:
        copy.wait()

    def halo_copy(lo, r):
        view = gathered.at[1, 1, lo, :, part_h]
        return remote(
            view, view, halo_send.at[r - 1], halo_recv.at[lo], in_row((x * 2 + core + r) % 8)
        )

    @pl.when(s == 3)
    def _():
        for r in range(1, 8):
            halo_copy(x_lo, r).start()

    all_tiles = ker_tiles.at[pl.ds(0, 31)]
    pltpu.make_async_copy(all_tiles, all_tiles, ker_recv).wait()
    w_copies = []
    for r in (2, 1, 3):
        w_copies.append(remote(
            taps.at[0, y], taps.at[0, y], w_send.at[r - 1], w_recv.at[r - 1], along_y(r)
        ))
        w_copies[-1].start()

    fetch.wait()
    turn_by = (128 - (inch % 4) * 32) % 128

    def widen(k, carry):
        at = pl.ds(pl.multiple_of(k * 256, 256), 256)
        resp_wide[at, :] = pltpu.roll(resp_raw[at, :].astype(F32), turn_by, axis=1)
        return carry

    lax.fori_loop(0, 8, widen, 0)

    def merge(parts, bit):
        lane = lax.broadcasted_iota(jnp.int32, parts[0].shape, 1)
        high = (lane & (8 * bit)) != 0
        return [
            jnp.where(high, pltpu.roll(parts[i | bit], 8 * bit, axis=1), parts[i])
            for i in range(len(parts)) if not i & bit
        ]

    def pack_response(b, carry):
        for half in range(2):
            parts = [
                resp_wide[pl.ds(b * 32 + half * 16 + p, 8, stride=256), :] for p in range(16)
            ]
            parts = merge(merge(parts, 8), 4)
            parts = swap_stage(swap_stage(parts, 1), 2)
            for g in range(4):
                resp_out[g, b, :, half * 128:(half + 1) * 128] = parts[g]
        return carry

    lax.fori_loop(0, 8, pack_response, 0)
    rows_s = pl.ds(pl.multiple_of(s * 8, 8), 8)
    resp_copies = []
    for r in (1, 2, 3):
        resp_copies.append(remote(
            resp_out.at[(s + r) % 4], response.at[:, rows_s, :],
            resp_send.at[r - 1], resp_recv.at[r - 1], in_group(r),
        ))
        resp_copies[-1].start()
    response[:, rows_s, :] = resp_out[s]

    cb_copies = []
    for r in (0, 1, 3, 2):
        there = (x + 4 - r) % 4
        if r:
            xa_copies[place[r]].wait_recv()
        if r:
            view = gathered.at[there // 2, core, there % 2, :, part_a]
            ca_copies.append(remote(view, view, ca_send.at[r], ca_recv.at[r], other))
            ca_copies[-1].start()
        for k in (1, 2, 3):
            zb_copies[r, k].wait_recv()
        view = gathered.at[there // 2, core, there % 2, :, part_b]
        cb_copies.append(remote(view, view, cb_send.at[r], cb_recv.at[r], other))
        cb_copies[-1].start()

    def upright(hi, of_core):
        def one(k, carry):
            for m in range(8):
                lanes = pl.ds(pl.multiple_of(256 + (k * 8 + m) * 128, 128), 128)
                block = jnp.concatenate(
                    [gathered[hi, of_core, 0, :, lanes], gathered[hi, of_core, 1, :, lanes]], axis=0
                )
                rows[hi * 2 + of_core, k * 8 + m] = block.T.astype(F32)
            return carry

        lax.fori_loop(0, 2, one, 0)

    for hi in range(2):
        upright(hi, core)
    for copy in ca_copies + cb_copies:
        copy.wait_recv()
    for hi in range(2):
        upright(hi, 1 - core)
    for lo in range(2):

        @pl.when(4 * (s // 3) + x_lo != 4 + lo)
        def _(lo=lo):
            halo_copy(lo, 1).wait_recv()

    at_start = y == 0
    for k in range(2):
        block = jnp.concatenate(
            [gathered[1, 1, lo, :, k * 128:(k + 1) * 128] for lo in range(2)], axis=0
        )
        halo[k * 128:(k + 1) * 128, :] = jnp.where(at_start, 0.0, block.astype(F32).T)
    for q in range(8):
        xe[:, q * 128:(q + 1) * 128] = halo[(7 - q) * 32:(8 - q) * 32, :].astype(BF16)
    first = lax.broadcasted_iota(jnp.int32, (32, 128), 0) == 0

    def order(p, carry):
        for b in range(8):
            at = pl.multiple_of((b % 4) * 32 + (p // 8) * 8, 8)
            block = jnp.concatenate(
                [rows[g, (p % 8) * 2 + b // 4, pl.ds(at, 8), :] for g in range(4)], axis=0
            )
            edge = jnp.broadcast_to(halo[pl.ds(b * 32 + p, 1), :], (32, 128))
            before = jnp.where(first, edge, pltpu.roll(block, 1, axis=0))
            sb[p, b * 32:(b + 1) * 32, :] = before.astype(BF16)
            sb[p, 256 + b * 32:256 + (b + 1) * 32, :] = block.astype(BF16)
        return carry

    lax.fori_loop(0, 32, order, 0)

    for copy in w_copies + resp_copies:
        copy.wait()

    wide_lane = lax.broadcasted_iota(jnp.int32, (256, 256), 1)
    wide_row = lax.broadcasted_iota(jnp.int32, (256, 256), 0)
    ext_lane = lax.broadcasted_iota(jnp.int32, (32, 256), 1)
    ext_row = lax.broadcasted_iota(jnp.int32, (32, 256), 0)

    def forward(turn):
        def tap_matrix():
            return jnp.concatenate([taps[turn, j] for j in range(4)], axis=0)

        lhs = jnp.concatenate(
            [
                jnp.concatenate(
                    [sb[p, (8 - q) * 32:(8 - q) * 32 + 256, :] for q in range(8)], axis=1
                )
                for p in range(32)
            ],
            axis=0,
        )
        product = jnp.dot(lhs, tap_matrix(), preferred_element_type=F32)
        here = product[0:256]
        after = jnp.zeros((256, 256), F32)
        for p in range(1, 32):
            turned = pltpu.roll(product[p * 256:(p + 1) * 256], 8 * p, axis=1)
            keep = wide_lane >= 8 * p
            here = here + jnp.where(keep, turned, 0.0)
            after = after + jnp.where(keep, 0.0, turned)
        edge = jnp.dot(xe[...], tap_matrix(), preferred_element_type=F32)
        edge = pltpu.roll(edge, 0, axis=1, stride=8, stride_axis=0)
        edge = jnp.sum(jnp.where(ext_lane < ext_row * 8, edge, 0.0), axis=0, keepdims=True)
        moved = jnp.where(
            wide_row >= 32, pltpu.roll(after, 32, axis=0), pltpu.roll(after, 33, axis=0)
        )
        moved = jnp.where(wide_row == 0, jnp.broadcast_to(edge, (256, 256)), moved)
        return (here + moved) * SCALE

    def expand(resid):
        here_t = resid.T
        later_t = jnp.where(
            wide_lane < 224, pltpu.roll(here_t, 224, axis=1), pltpu.roll(here_t, 223, axis=1)
        )
        later_t = jnp.where(wide_lane == 255, 0.0, later_t)
        both = jnp.concatenate([here_t, later_t], axis=0)
        r_even[...] = both.astype(BF16)
        r_odd[...] = jnp.concatenate([both[8:], both[:8]], axis=0).astype(BF16)

    def edge_windows(resid):
        line = jnp.broadcast_to(resid[0:1, :], (32, 256))
        line = pltpu.roll(line, 8, axis=1, stride=8, stride_axis=0)
        return jnp.where(ext_lane + (31 - ext_row) * 8 >= 256, line, 0.0)

    def gradient_of(one, two, edges):
        total = jnp.zeros((256, 256), F32)
        first_at = pl.multiple_of((8 - one) * 32, 32)
        second_at = pl.multiple_of((8 - two) * 32, 32)
        for g in range(8):
            left = []
            right = []
            for p in range(4 * g, 4 * g + 4):
                windows = r_odd if p % 2 else r_even
                at = 8 * (p - p % 2)
                left.append(windows[at:at + 256, :])
                right.append(jnp.concatenate(
                    [sb[p, pl.ds(first_at, 256), :], sb[p, pl.ds(second_at, 256), :]], axis=1
                ))
            total = total + jnp.dot(
                jnp.concatenate(left, axis=1), jnp.concatenate(right, axis=0),
                preferred_element_type=F32,
            )
        edge_rows = jnp.concatenate(
            [
                xe[:, pl.ds(pl.multiple_of(one * 128, 128), 128)],
                xe[:, pl.ds(pl.multiple_of(two * 128, 128), 128)],
            ],
            axis=1,
        )
        total = total + jnp.dot(edges, edge_rows, preferred_element_type=F32)
        return total.T * SCALE

    def send_energy(turn):
        energy_own[turn, 0] = jnp.full((8, 128), jnp.sum(grad_own[...] * grad_own[...]), F32)

        def send(r, carry):
            remote(
                energy_own.at[turn, 0], energy_a.at[turn, r - 1],
                ea_send.at[turn], ea_recv.at[turn], in_plane((rank + r) % 32),
            ).start()
            return carry

        lax.fori_loop(1, 32, send, 0)

    def send_tiles(turn):

        def send(r, carry):
            d = (rank + r) % 32
            to = d // 4
            rows_d = pl.multiple_of(((d % 4) // 2) * 128 + (to % 2) * 64 + (to // 2) * 16, 16)
            lanes = pl.ds(pl.multiple_of((d % 2) * 128, 128), 128)
            remote(
                taps.at[turn + 1, y, pl.ds(rows_d, 16), lanes], tiles.at[turn, rank],
                t_send.at[turn], t_recv.at[turn], in_plane(d),
            ).start()
            return carry

        lax.fori_loop(1, 32, send, 0)
        tiles[turn, rank] = taps[turn + 1, y, pl.ds(row_k, 16), pl.ds(lane_k, 128)]

    def energy_copy(turn, r):
        return remote(
            energy_own.at[turn, 1], energy_b.at[turn, r - 1],
            eb_send.at[turn, r - 1], eb_recv.at[turn, r - 1], along_y(r),
        )

    def pass_energy(turn):
        mine = energy_a.at[turn]
        pltpu.make_async_copy(mine, mine, ea_recv.at[turn]).wait()
        energy_own[turn, 1] = energy_own[turn, 0] + jnp.sum(energy_a[turn], axis=0)
        for r in (1, 2, 3):
            energy_copy(turn, r).start()

    def finish_energy(turn):
        for r in (1, 2, 3):
            energy_copy(turn, r).wait()
        total = energy_own[turn, 1] + jnp.sum(energy_b[turn], axis=0)
        factor_rows[turn + 1] = STEP_SIZE * lax.rsqrt(total / COUNT + EPSILON)

    def resid_copy(r):
        there = pl.ds(pl.multiple_of(((s + r) % 4) * 8, 8), 8)
        return remote(
            resid_all.at[:, there, :], resid_in.at[s],
            o_send.at[r - 1], o_recv.at[r - 1], in_group(r),
        )

    def shard_copy(turn, half, r):
        at = pl.ds(pl.multiple_of(half * 128, 128), 128)
        return remote(
            grad_out.at[r - 1, at], grad_in.at[r - 1, at],
            rs_send.at[turn, half, r - 1], rs_recv.at[turn, half, r - 1], along_y(r),
        )

    def gather_copy(half, r):
        view = taps.at[1, y, pl.ds(half * 128, 128)]
        return remote(view, view, ag_send.at[half, r - 1], ag_recv.at[half, r - 1], along_y(r))

    base[...] = jnp.zeros_like(base)
    factor_rows[0] = jnp.ones((8, 128), F32)

    def iterate(turn, carry):
        change = forward(turn)

        @pl.when(turn == 1)
        def _():
            finish_energy(0)

        factor = factor_rows[turn, 0:1, :]
        predicted = base[...] + jnp.concatenate([factor, factor], axis=1) * change
        base[...] = predicted
        resid = (response[...].reshape(256, 256) - predicted).astype(BF16).astype(F32)

        @pl.when(turn == 1)
        def _():
            resid_all[...] = resid.reshape(8, 32, 256)
            for r in (1, 2, 3):
                resid_copy(r).start()
            resid_in[s] = resid_all[:, rows_s, :]

        expand(resid)
        flipped = edge_windows(resid)
        edge_t[...] = jnp.concatenate(
            [flipped[31 - j:32 - j, :] for j in range(32)], axis=0
        ).T.astype(BF16)

        def chunk(j, carry):
            half = j // 2
            late = j % 2
            ahead = 2 + late
            beside = 1 - late
            part = gradient_of(
                (y + ahead) % 4 * 2 + half, (y + beside) % 4 * 2 + half, edge_t[...]
            )
            at = pl.ds(pl.multiple_of(half * 128, 128), 128)
            grad_out[ahead - 1, at] = part[0:128].astype(BF16)
            shard_copy(turn, half, ahead).start()

            @pl.when(late == 0)
            def _():
                grad_out[0, at] = part[128:256].astype(BF16)
                shard_copy(turn, half, 1).start()

            @pl.when(late == 1)
            def _():
                grad_own[at, :] = part[128:256]

            return carry

        lax.fori_loop(0, 4, chunk, 0)

        @pl.when(turn == 1)
        def _():
            send_tiles(0)

        for half in range(2):
            at = slice(half * 128, (half + 1) * 128)
            for r in (1, 2, 3):
                shard_copy(turn, half, r).wait()
            own = grad_own[at, :]
            for r in range(3):
                own = own + grad_in[r, at].astype(F32)
            grad_own[at, :] = own
            taps[turn + 1, y, at] = own.astype(BF16)

            @pl.when(turn == 0)
            def _(half=half):
                for r in (2, 1, 3):
                    gather_copy(half, r).start()

        send_energy(turn)

        @pl.when(turn == 1)
        def _():
            send_tiles(1)

        pass_energy(turn)

        @pl.when(turn == 0)
        def _():
            for half in range(2):
                for r in (1, 3, 2):
                    gather_copy(half, r).wait()

        return carry

    lax.fori_loop(0, 2, iterate, 0)

    for r in (1, 2, 3):
        resid_copy(r).wait()

    def unpack_residual(b, carry):
        for half in range(2):
            parts = [resid_in[g, b, :, half * 128:(half + 1) * 128] for g in range(4)]
            parts = swap_stage(swap_stage(parts, 1), 2)
            for m in range(4):
                for l in range(4):
                    part = parts[l] if m == 0 else pltpu.roll(parts[l], 128 - 32 * m, axis=1)
                    at = b * 32 + half * 16 + 4 * m + l
                    resid_wide[pl.ds(at, 8, stride=256), :] = part
        return carry

    lax.fori_loop(0, 8, unpack_residual, 0)
    for k in range(16):
        flat = resid_wide[k * 128:(k + 1) * 128, :].T
        resid_ref[:, k * 128:(k + 1) * 128] = flat[0:32, :].astype(BF16)

    for turn in range(2):
        half = tiles.at[turn, pl.ds(0, 31)]
        pltpu.make_async_copy(half, half, t_recv.at[turn]).wait()
    moved = []
    for half in range(2):
        for turn in range(2):
            moved.append(swap_blocks(
                [tiles[turn, half * 16 + d].astype(F32) for d in range(16)]
            ))
    for half in range(2):
        lanes = slice(half * 128, (half + 1) * 128)
        for u in range(16):
            kernel_ref[u, :, lanes] = factor_rows[1, 0:1, :] * moved[2 * half][u]
            ker_ref[u, :, lanes] = moved[2 * half + 1][u]
    finish_energy(1)
    last = factor_rows[2, 0:1, :]
    wide_last = jnp.concatenate([last, last], axis=1)
    for u in range(16):
        kernel_ref[u] = kernel_ref[u] + wide_last * ker_ref[u]

    pltpu.make_async_copy(all_tiles, all_tiles, ker_send).wait()
    for copy in za_copies + xb_copies + xa_copies + ca_copies + cb_copies:
        copy.wait_send()

    @pl.when(s == 3)
    def _():
        for r in range(1, 8):
            halo_copy(x_lo, r).wait_send()

    for copy in zb_copies.values():
        copy.wait_send()
    for turn in range(2):
        mine = energy_a.at[turn]
        pltpu.make_async_copy(mine, mine, ea_send.at[turn]).wait()
        half = tiles.at[turn, pl.ds(0, 31)]
        pltpu.make_async_copy(half, half, t_send.at[turn]).wait()


def finish(step_ref, ker_ref, resid_in_ref, kernel_ref, resid_ref):
    kernel_ref[...] = ker_ref[...] + step_ref[...]
    resid_ref[...] = resid_in_ref[...]


def local(signal, response, kernel):
    dma = pltpu.SemaphoreType.DMA
    vmem = pl.BlockSpec(memory_space=pltpu.VMEM)
    kernel_out, resid = pl.pallas_call(
        body,
        out_shape=(
            jax.ShapeDtypeStruct((16, 16, 256), F32),
            jax.ShapeDtypeStruct((32, 2048), BF16),
        ),
        in_specs=[pl.BlockSpec(memory_space=pl.ANY)] * 3,
        out_specs=(vmem, vmem),
        scratch_shapes=[
            pltpu.VMEM((2, 2, 2, 64, 2304), BF16),
            pltpu.VMEM((4, 16, 128, 128), F32),
            pltpu.VMEM((256, 128), F32),
            pltpu.VMEM((32, 16, 128), BF16),
            pltpu.VMEM((2048, 128), BF16),
            pltpu.VMEM((2048, 128), F32),
            pltpu.VMEM((4, 8, 8, 256), F32),
            pltpu.VMEM((2048, 128), F32),
            pltpu.VMEM((256, 256), F32),
            pltpu.VMEM((32, 512, 128), BF16),
            pltpu.VMEM((32, 1024), BF16),
            pltpu.VMEM((3, 4, 256, 256), BF16),
            pltpu.VMEM((8, 32, 256), F32),
            pltpu.VMEM((512, 256), BF16),
            pltpu.VMEM((512, 256), BF16),
            pltpu.VMEM((3, 256, 256), BF16),
            pltpu.VMEM((3, 256, 256), BF16),
            pltpu.VMEM((256, 256), F32),
            pltpu.VMEM((2, 32, 16, 128), BF16),
            pltpu.VMEM((3, 8, 128), F32),
            pltpu.VMEM((2, 31, 8, 128), F32),
            pltpu.VMEM((2, 3, 8, 128), F32),
            pltpu.VMEM((2, 2, 8, 128), F32),
            pltpu.VMEM((8, 32, 256), F32),
            pltpu.VMEM((4, 8, 8, 256), F32),
            pltpu.VMEM((256, 32), BF16),
            pltpu.VMEM((16, 2048), BF16),
            pltpu.VMEM((16, 16, 256), F32),
            dma((2,)),
            dma, dma, dma, dma((3,)), dma((3,)), dma((4,)), dma((4,)),
            dma((3,)), dma((3,)), dma((3,)), dma((3,)), dma((3,)), dma((3,)),
            dma((7,)), dma((2,)), dma((4, 3)), dma((4, 3)), dma((4,)), dma((4,)), dma((4,)), dma((4,)),
            dma((3,)), dma((3,)), dma((2, 2, 3)), dma((2, 2, 3)), dma((2, 3)), dma((2, 3)),
            dma((2,)), dma((2,)), dma((2, 3)), dma((2, 3)), dma((2,)), dma((2,)), dma((3,)), dma((3,)),
        ],
        compiler_params=pltpu.CompilerParams(
            collective_id=0, has_side_effects=True, vmem_limit_bytes=60 * 2**20
        ),
    )(signal.T, response, kernel)
    kernel_out, resid = pl.pallas_call(
        finish,
        out_shape=(
            jax.ShapeDtypeStruct((16, 16, 256), F32),
            jax.ShapeDtypeStruct((32, 2048), BF16),
        ),
        in_specs=[vmem] * 3,
        out_specs=(vmem, vmem),
    )(kernel_out, kernel, resid)
    return kernel_out, resid.T


def solution(mesh):
    placed = (P("tm", "inch"), P("tm", None), P("tm", "inch", None))
    return jax.shard_map(
        local,
        mesh=mesh,
        in_specs=placed,
        out_specs=(P("tm", "inch", None), P("tm", "inch")),
        check_vma=False,
    )
```
